32 devices in a mesh: grp: 2 (over y), seq: 4 (over x, core), tp: 4 (over z).
Axes of the slice: x: 2, y: 2, z: 4, core: 2. Of those that a mesh axis runs over, the one named last changes fastest.
Arguments:
- fc_big: bfloat16 [1024, 6912], P(('grp', 'seq'), 'tp'), may hold values from -6 to 6
- fc_guide: bfloat16 [1024, 4480], P(('grp', 'seq'), 'tp'), may hold values from -6 to 6
- res_big: bfloat16 [1024, 5120], P(('grp', 'tp'), 'seq'), may hold values from -6 to 6
- res_guide: bfloat16 [1024, 1536], P(('grp', 'tp'), 'seq'), may hold values from -6 to 6
- cotangent: float32 [1024, 64], P(('grp', 'tp')), may hold values from -6 to 6
- proj_big: bfloat16 [6912, 5120], P('tp', 'seq'), may hold values from -0.078125 to 0.078125
- proj_guide: bfloat16 [4480, 1536], P('tp', 'seq'), may hold values from -0.09375 to 0.09375
- head_big: bfloat16 [5120, 64], P('seq'), may hold values from -0.078125 to 0.078125
- head_guide: bfloat16 [1536, 64], P('seq'), may hold values from -0.15625 to 0.15625
- modulation_big: float32 [50, 3, 5120], P(None, None, 'seq'), may hold values from -3 to 3
- modulation_guide: float32 [50, 3, 1536], P(None, None, 'seq'), may hold values from -3 to 3
- weight_table: float32 [8], replicated, may hold values from 1.5 to 4
- time_index: int32 [2], P('grp'), may hold values from 0 to 49
- weight_index: int32 [2], P('grp'), may hold values from 0 to 7
Outputs:
- guided: float32 [1024, 64], P(('grp', 'tp'))
- grad_proj: bfloat16 [6912, 5120], P('tp', 'seq')
- grad_head: float32 [5120, 64], P('seq')
- grad_res_big: bfloat16 [1024, 5120], P(('grp', 'tp'), 'seq')
- grad_res_guide: bfloat16 [1024, 1536], P(('grp', 'tp'), 'seq')
The draws below stay inside these ranges and needn't reach their ends.
All inputs are finite; a program needn't handle non-finite values.
Results may differ from the reference program's by a relative error of at most 0.019.
Values may be sent and summed in bfloat16 or wider, within the bound.
No kernel may reach another device: no remote copies, remote signals or barrier semaphores. Data moves between devices by JAX's collectives and lax.ppermute only.
A program may use at most 64 MiB of HBM per device.

```python
import jax
import jax.numpy as jnp
from jax import lax

DB = 5120
FFB = 6912
DG = 1536
FFG = 4480
PATCH = 64
STEPS = 50
LEVELS = 8
GROUP_TOKENS = 512
TOKENS = 1024
SAMPLES = 2
N_GRP = 2
N_TP = 4


def shard_levels(own_key, shape, shards, low, largest):
    level, own = 1.0, jax.random.fold_in(own_key, 6)
    for position, blocks in shards:
        heights = jnp.exp(jax.random.uniform(jax.random.fold_in(own, position), (blocks,), jnp.float32, low / len(shards), largest / len(shards)))
        level = level * jnp.repeat(heights, shape[position] // blocks).reshape([-1 if axis == position else 1 for axis in range(len(shape))])
    return level


def noise(stream_key, extent, deviation, reach, pieces=(), kind=jnp.bfloat16):
    entries = deviation * jax.random.normal(stream_key, extent, jnp.float32)
    if pieces:
        entries = entries * shard_levels(stream_key, extent, pieces, -0.22, 0.18)
    return jnp.clip(entries, -reach, reach).astype(kind)


def setup_inputs(seed: int = 0) -> dict:
    splits = jax.random.split(jax.random.key(seed), 15)
    return {
        "fc_big": noise(splits[0], (TOKENS, FFB), 1.0, 6.0, ((0, 8), (1, 4))),
        "fc_guide": noise(splits[1], (TOKENS, FFG), 1.0, 6.0, ((0, 8), (1, 4))),
        "res_big": noise(splits[2], (TOKENS, DB), 1.0, 6.0, ((0, 8), (1, 4))),
        "res_guide": noise(splits[3], (TOKENS, DG), 1.0, 6.0, ((0, 8), (1, 4))),
        "cotangent": noise(splits[4], (TOKENS, PATCH), 1.0, 6.0, ((0, 8),), jnp.float32),
        "proj_big": noise(splits[5], (FFB, DB), FFB ** -0.5, 0.078125, ((0, 4), (1, 4))),
        "proj_guide": noise(splits[6], (FFG, DG), FFG ** -0.5, 0.09375, ((0, 4), (1, 4))),
        "head_big": noise(splits[7], (DB, PATCH), DB ** -0.5, 0.078125, ((0, 4),)),
        "head_guide": noise(splits[8], (DG, PATCH), DG ** -0.5, 0.15625, ((0, 4),)),
        "modulation_big": noise(splits[9], (STEPS, 3, DB), 0.5, 3.0, ((2, 4),), jnp.float32),
        "modulation_guide": noise(splits[10], (STEPS, 3, DG), 0.5, 3.0, ((2, 4),), jnp.float32),
        "weight_table": jnp.clip(jax.random.uniform(splits[11], (LEVELS,), jnp.float32, 1.5, 4.0), 1.5, 4.0),
        "time_index": jax.random.randint(splits[12], (SAMPLES,), 0, STEPS).astype(jnp.int32),
        "weight_index": jax.random.randint(splits[13], (SAMPLES,), 0, LEVELS).astype(jnp.int32),
    }


EPSILON = 1e-06

def split_sum(hidden, weight):
    stride = weight.shape[0] // N_TP
    running = jnp.zeros((hidden.shape[0], weight.shape[1]), jnp.float32)
    for segment in range(N_TP):
        portion = jnp.dot(hidden[:, segment * stride:(segment + 1) * stride], weight[segment * stride:(segment + 1) * stride], preferred_element_type=jnp.float32)
        rounded = lax.optimization_barrier(portion.astype(jnp.bfloat16))
        running = running + rounded.astype(jnp.float32)
    return running

def forward_model(hidden, stream_in, weight, table_row):
    summed = split_sum(hidden, weight)
    stream = stream_in.astype(jnp.float32) + table_row[0] * summed
    centre = lax.optimization_barrier(jnp.mean(stream, axis=1, keepdims=True))
    centred = stream - centre
    variance = lax.optimization_barrier(jnp.mean(centred * centred, axis=1, keepdims=True))
    inverse_std = lax.rsqrt(variance + EPSILON)
    normed = centred * inverse_std
    shaped = (normed * (1.0 + table_row[2]) + table_row[1]).astype(jnp.bfloat16)
    return (normed, inverse_std, shaped)

def backward_norm(cot_rows, head, table_row, normed, inverse_std):
    upstream = jnp.dot(cot_rows, head.T, preferred_element_type=jnp.float32)
    scaled = upstream * (1.0 + table_row[2])
    first_mean = lax.optimization_barrier(jnp.mean(scaled, axis=1, keepdims=True))
    second_mean = lax.optimization_barrier(jnp.mean(scaled * normed, axis=1, keepdims=True))
    return inverse_std * (scaled - first_mean - normed * second_mean)

def reference(fc_big, fc_guide, res_big, res_guide, cotangent, proj_big, proj_guide, head_big, head_guide, modulation_big, modulation_guide, weight_table, time_index, weight_index):

    def sample_step(running, sample_slices):
        hidden_big, hidden_guide, stream_big, stream_guide, cotangent_rows, time_value, level_value = sample_slices
        strength = weight_table[level_value]
        table_big = modulation_big[time_value]
        table_guide = modulation_guide[time_value]
        normed_big, inverse_big, shaped_big = forward_model(hidden_big, stream_big, proj_big, table_big)
        normed_guide, inverse_guide, shaped_guide = forward_model(hidden_guide, stream_guide, proj_guide, table_guide)
        out_big = jnp.dot(shaped_big, head_big, preferred_element_type=jnp.float32)
        out_guide = jnp.dot(shaped_guide, head_guide, preferred_element_type=jnp.float32)
        guided_rows = out_guide + strength * (out_big - out_guide)
        cot_big = (strength * cotangent_rows).astype(jnp.bfloat16)
        cot_guide = ((1.0 - strength) * cotangent_rows).astype(jnp.bfloat16)
        grad_big = backward_norm(cot_big, head_big, table_big, normed_big, inverse_big)
        grad_guide = backward_norm(cot_guide, head_guide, table_guide, normed_guide, inverse_guide)
        signal = (grad_big * table_big[0]).astype(jnp.bfloat16)
        proj_part = jnp.dot(hidden_big.T, signal, preferred_element_type=jnp.float32)
        head_part = jnp.dot(shaped_big.T, cot_big, preferred_element_type=jnp.float32)
        return ((running[0] + proj_part, running[1] + head_part), (guided_rows, grad_big.astype(jnp.bfloat16), grad_guide.astype(jnp.bfloat16)))
    sample_slices = (fc_big.reshape(N_GRP, GROUP_TOKENS, FFB), fc_guide.reshape(N_GRP, GROUP_TOKENS, FFG), res_big.reshape(N_GRP, GROUP_TOKENS, DB), res_guide.reshape(N_GRP, GROUP_TOKENS, DG), cotangent.reshape(N_GRP, GROUP_TOKENS, PATCH), time_index, weight_index)
    initial = (jnp.zeros((FFB, DB), jnp.float32), jnp.zeros((DB, PATCH), jnp.float32))
    totals, stacked = lax.scan(sample_step, initial, sample_slices)
    guided = stacked[0].reshape(TOKENS, PATCH)
    grad_res_big = stacked[1].reshape(TOKENS, DB)
    grad_res_guide = stacked[2].reshape(TOKENS, DG)
    return (guided, totals[0].astype(jnp.bfloat16), totals[1], grad_res_big, grad_res_guide)
```

```python
import functools

import jax
import jax.numpy as jnp
from jax import lax
from jax.experimental import pallas as pl
from jax.experimental.pallas import tpu as pltpu
from jax.sharding import PartitionSpec as P

EPSILON = 1e-06
F32 = jnp.float32
BF16 = jnp.bfloat16
VMEM = 40 * 1024 * 1024
VMEM_NORM = 24 * 1024 * 1024
VMEM_SMALL = 8 * 1024 * 1024
SHORT = pl.CostEstimate(flops=0, bytes_accessed=0, transcendentals=0)


def swap(x, axis, size, bits):
    return lax.ppermute(x, axis, [(i, i ^ bits) for i in range(size)])


def near_far(block, n, later=()):
    far = [swap(after(block, later), "seq", n, k) for k in range(2, n, 2)]
    return [block, swap(block, "seq", n, 1)], far


def forward(far, n, later=()):
    return [x for block in far for x in (block, swap(after(block, later), "seq", n, 1))]


def gather_direct(block, axis, n):
    return [block] + [swap(block, axis, n, j) for j in range(1, n)]


def after(x, *others):
    return lax.optimization_barrier((x, others))[0]


def gather_pairs(block):
    pairs = [(4 * g + t, 4 * (1 - g) + (t ^ 1)) for g in range(2) for t in range(4)]
    two = swap(block, "tp", 4, 2)
    across = swap(block, "grp", 2, 1)
    across_one = lax.ppermute(block, ("grp", "tp"), pairs)
    two = lax.optimization_barrier((across_one, across, two))[2]
    three = swap(two, "tp", 4, 1)
    across_two = swap(two, "grp", 2, 1)
    three = after(three, across_two)
    across_three = swap(three, "grp", 2, 1)
    one = swap(after(block, two), "tp", 4, 1)
    return [block, one, two, three], [across, across_one, across_two, across_three]


def add_kernel(left, right, out):
    out[...] = (left[...].astype(F32) + right[...].astype(F32)).astype(BF16)


def add(left, right):
    return pl.pallas_call(
        add_kernel,
        out_shape=jax.ShapeDtypeStruct(left.shape, BF16),
        compiler_params=pltpu.CompilerParams(vmem_limit_bytes=VMEM_SMALL),
        cost_estimate=SHORT,
        name="add",
    )(left, right)


def scatter(terms, n):
    if n != 4:
        return [terms[0]] + [swap(terms[k], "tp", n, k) for k in range(1, n)], terms[0]
    joined = add(terms[2], swap(terms[3], "tp", n, 1))
    return [terms[0], swap(terms[1], "tp", n, 1), swap(joined, "tp", n, 2)], joined


def lookup_kernel(count, *refs):
    steps, tables, outs = refs[:count], refs[count : 2 * count], refs[2 * count :]
    for step, table, out in zip(steps, tables, outs):
        for row in range(3):
            out[row : row + 1, :] = table[row, pl.ds(step[0], 1), :]


def lookup(tables, steps):
    turned = [jnp.transpose(table, (1, 0, 2)) for table in tables]
    count = len(tables)
    return pl.pallas_call(
        functools.partial(lookup_kernel, count),
        in_specs=[pl.BlockSpec(memory_space=pltpu.SMEM)] * count
        + [pl.BlockSpec(memory_space=pltpu.VMEM)] * count,
        out_shape=[jax.ShapeDtypeStruct((3, t.shape[2]), F32) for t in turned],
        compiler_params=pltpu.CompilerParams(vmem_limit_bytes=VMEM_SMALL),
        cost_estimate=SHORT,
        name="lookup",
    )(*steps, *turned)


def total(parts):
    return sum(p.astype(F32) for p in parts)


def meeting():
    return jnp.bitwise_xor(lax.axis_index("seq"), lax.axis_index("tp"))


def turned_dot(left, right):
    return lax.dot_general(left, right, (((0,), (0,)), ((), ())), preferred_element_type=F32)


def whole_block(x):
    return pl.BlockSpec(x.shape, lambda i: (0,) * x.ndim)


def project_kernel(last, filled, n, *refs):
    blocks, weight = refs[:n], refs[n]
    rows = blocks[0].shape[1]
    left = refs[-2] if last else refs[-1]

    @pl.when(pl.program_id(0) == 0)
    def _():
        for j in range(n):
            left[j * rows : (j + 1) * rows, :] = blocks[j][...].T

    product = jnp.dot(left[...], weight[...], preferred_element_type=F32).astype(BF16)
    if not last:
        refs[n + 1][...] = product
        return
    every = refs[-1]
    earlier = refs[n + 1].shape[0]
    total_blocks = n + earlier // rows
    every[:earlier, :] = refs[n + 1][...]
    every[earlier:, :] = product
    outs = refs[n + 2 + filled * total_blocks : -2]
    turn = meeting()
    for k in range(total_blocks):
        start = pl.multiple_of(jnp.bitwise_xor(turn, k) * rows, rows)
        outs[k][...] = every[pl.ds(start, rows), :]


def project_early(blocks, weight, tile):
    n = len(blocks)
    depth, columns = weight.shape
    rows = blocks[0].shape[0]
    turned = [block.T for block in blocks]
    return pl.pallas_call(
        functools.partial(project_kernel, False, False, n),
        grid=(pl.cdiv(columns, tile),),
        in_specs=[whole_block(t) for t in turned] + [pl.BlockSpec((depth, tile), lambda i: (0, i))],
        out_specs=pl.BlockSpec((n * rows, tile), lambda i: (0, i)),
        out_shape=jax.ShapeDtypeStruct((n * rows, columns), BF16),
        scratch_shapes=[pltpu.VMEM((n * rows, depth), BF16)],
        compiler_params=pltpu.CompilerParams(vmem_limit_bytes=VMEM),
        cost_estimate=SHORT,
        name="project_early",
    )(*turned, weight)


def project(blocks, weight, tile, width, early, before=()):
    n = len(blocks)
    depth, columns = weight.shape
    rows = blocks[0].shape[0]
    owners = n + early.shape[0] // rows
    turned = [block.T for block in blocks]
    first = (width - columns) // tile if before else 0
    anywhere = pl.BlockSpec(memory_space=pl.ANY)
    return pl.pallas_call(
        functools.partial(project_kernel, True, bool(before), n),
        grid=(pl.cdiv(columns, tile),),
        in_specs=[whole_block(t) for t in turned]
        + [pl.BlockSpec((depth, tile), lambda i: (0, i))]
        + [pl.BlockSpec((early.shape[0], tile), lambda i: (0, i))]
        + [anywhere] * len(before),
        out_specs=[pl.BlockSpec((rows, tile), lambda i: (0, first + i)) for _ in range(owners)],
        out_shape=[jax.ShapeDtypeStruct((rows, width), BF16) for _ in range(owners)],
        input_output_aliases={n + 2 + k: k for k in range(len(before))},
        scratch_shapes=[
            pltpu.VMEM((n * rows, depth), BF16),
            pltpu.VMEM((owners * rows, tile), BF16),
        ],
        compiler_params=pltpu.CompilerParams(vmem_limit_bytes=VMEM),
        cost_estimate=SHORT,
        name="project",
    )(*turned, weight, early, *before)


def contract_kernel(n, counts, more, *refs):
    refs = list(refs)
    take = lambda count: [refs.pop(0) for _ in range(count)]
    samples = [(take(n), take(len(slots)), *take(1)) for slots in counts]
    (head,) = take(1)
    before = take(2) if more else None
    out, head_out, signal, shelf, done = refs
    patch, rows, tile = head.shape[0], shelf.shape[2], out.shape[0]
    turn = meeting()
    wanted = [(hidden, k) for slots, (hidden, *_) in zip(counts, samples) for k in slots]

    @pl.when(pl.program_id(0) == 0)
    def _():
        for place, (hidden, k) in enumerate(wanted):
            for j in range(n):

                @pl.when(jnp.bitwise_xor(turn, k) == j)
                def _():
                    pltpu.make_async_copy(hidden[j], shelf.at[place], done.at[place]).start()

        gradient = before[1][...] if more else jnp.zeros(head_out.shape, F32)
        place = 0
        for _, sent, table in samples:
            gate, shift, scale = table[0:1, :], table[1:2, :], 1.0 + table[2:3, :]
            for ref in sent:
                block = ref[...].astype(F32)
                normed = block[:rows]
                pieces = [
                    block[r : r + 8, c : c + rows]
                    for r in range(rows, block.shape[0], 8)
                    for c in range(0, block.shape[1] - rows + 1, rows)
                ]
                sums = pieces[0] + jnp.concatenate([pieces[0][3:], pieces[0][:3]], axis=0)
                sums = sums.T
                cot = jnp.concatenate(pieces[1 : 1 + patch // 8], axis=0).astype(BF16)
                inverse, first, second = sums[:, 0:1], sums[:, 1:2], sums[:, 2:3]
                scaled = turned_dot(cot, head[...]) * scale
                grad = inverse * (scaled - first - normed * second)
                signal[place : place + rows, :] = (grad * gate).astype(BF16)
                shaped = (normed * scale + shift).astype(BF16)
                gradient = gradient + jnp.dot(cot, shaped, preferred_element_type=F32)
                place += rows
        head_out[...] = gradient
        for place, (hidden, _) in enumerate(wanted):
            pltpu.make_async_copy(hidden[0], shelf.at[place], done.at[place]).wait()

    here = pl.ds(pl.multiple_of(pl.program_id(0) * tile, tile), tile)
    left = jnp.concatenate([shelf[place, here, :] for place in range(len(wanted))], axis=1)
    product = jnp.dot(left, signal[...], preferred_element_type=F32)
    if more:
        product = product + before[0][here, :].astype(F32)
    out[...] = product.astype(BF16)


def contract(samples, head, before=None):
    n = len(samples[0][0])
    counts = [tuple(slots) for _, slots, *_ in samples]
    tokens, depth = samples[0][0][0].shape
    width = head.shape[1]
    tile = max(t for t in range(16, min(depth, 576) + 1, 16) if depth % t == 0)
    operands, in_specs = [], []
    for hidden, slots, sent, table in samples:
        operands += [block.T for block in hidden]
        in_specs += [pl.BlockSpec(memory_space=pl.ANY) for _ in range(n)]
        rest = [*(sent[k] for k in slots), table]
        operands += rest
        in_specs += [whole_block(x) for x in rest]
    operands.append(head)
    in_specs.append(whole_block(head))
    if before is not None:
        operands += before
        in_specs += [pl.BlockSpec(memory_space=pltpu.VMEM), whole_block(before[1])]
    return pl.pallas_call(
        functools.partial(contract_kernel, n, counts, before is not None),
        grid=(depth // tile,),
        in_specs=in_specs,
        out_specs=[pl.BlockSpec((tile, width), lambda i: (i, 0)), whole_block(head)],
        out_shape=[
            jax.ShapeDtypeStruct((depth, width), BF16),
            jax.ShapeDtypeStruct(head.shape, F32),
        ],
        scratch_shapes=[
            pltpu.VMEM((sum(map(len, counts)) * tokens, width), BF16),
            pltpu.VMEM((sum(map(len, counts)), depth, tokens), BF16),
            pltpu.SemaphoreType.DMA((sum(map(len, counts)),)),
        ],
        compiler_params=pltpu.CompilerParams(vmem_limit_bytes=VMEM),
        cost_estimate=SHORT,
        name="contract",
    )(*operands)


def lanes(shape):
    return lax.broadcasted_iota(jnp.int32, shape, 1)


def model_stats(summed, res, table, head, cot):
    patch, rows = cot.shape
    gate, shift, scale = table[0:1, :], table[1:2, :], 1.0 + table[2:3, :]
    stream = res[...].astype(F32) + gate * summed
    scaled = turned_dot(cot.astype(BF16), head[...]) * scale
    mean = jnp.mean(stream, axis=1, keepdims=True)
    centred = stream - mean
    columns = [
        mean,
        jnp.sum(centred * centred, axis=1, keepdims=True),
        jnp.sum(scaled, axis=1, keepdims=True),
        jnp.sum(scaled * centred, axis=1, keepdims=True),
    ]
    lane = lanes((rows, rows))
    spread = jnp.zeros((rows, rows), F32)
    for place, column in enumerate(columns):
        spread = jnp.where(lane == place, column, spread)
    first = spread.T[:8]
    wide = head[...].astype(F32)
    slope = jnp.sum(wide * scale, axis=1, keepdims=True)
    offset = jnp.sum(wide * shift, axis=1, keepdims=True)
    lane, row = lanes((patch, rows)), lax.broadcasted_iota(jnp.int32, (patch, rows), 0)
    both = jnp.where(lane == row, slope, jnp.where(lane == row + patch, offset, 0.0))
    both = jnp.sum(both, axis=0, keepdims=True)
    first = jnp.where(lax.broadcasted_iota(jnp.int32, (8, rows), 0) == len(columns), both, first)
    product = lax.dot_general(
        head[...], (centred * scale).astype(BF16), (((1,), (1,)), ((), ())), preferred_element_type=F32
    )
    return stream, scaled, jnp.concatenate([first, product], axis=0)


def stats_kernel(n, *refs):
    big, guide = refs[n : n + 3], refs[n + 3 : n + 6]
    cot, strength = refs[n + 6][...], refs[n + 7][refs[n + 8][0]]
    stream_big, scaled_big, stream_guide, scaled_guide, told = refs[n + 9 :]
    summed = total([ref[...] for ref in refs[:n]])
    width = big[0].shape[1]
    stream_big[...], scaled_big[...], told_big = model_stats(summed[:, :width], *big, strength * cot)
    stream_guide[...], scaled_guide[...], told_guide = model_stats(
        summed[:, width:], *guide, (1.0 - strength) * cot
    )
    left = jnp.concatenate([told_big[:8], told_guide[:8]], axis=0)
    parts = []
    for _ in range(3):
        parts.append(left.astype(BF16).astype(F32))
        left = left - parts[-1]
    told[...] = jnp.concatenate([*parts, told_big[8:], told_guide[8:]], axis=0).astype(BF16)


def specs(arrays):
    return [pl.BlockSpec(memory_space=pltpu.VMEM) for _ in arrays] + [
        pl.BlockSpec(memory_space=pltpu.SMEM) for _ in range(2)
    ]


def local_stats(received, big, guide, cot, weight):
    patch, rows = cot.shape
    widths = [model[-1].shape[1] for model in (big, guide)]
    shapes = [(rows, w) for w in widths for _ in range(2)]
    arrays = [*received, *big, *guide, cot]
    return pl.pallas_call(
        functools.partial(stats_kernel, len(received)),
        in_specs=specs(arrays),
        out_shape=[jax.ShapeDtypeStruct(shape, F32) for shape in shapes]
        + [jax.ShapeDtypeStruct((48 + 2 * patch, rows), BF16)],
        compiler_params=pltpu.CompilerParams(vmem_limit_bytes=VMEM_NORM),
        cost_estimate=SHORT,
        name="local_stats",
    )(*arrays, *weight)


def model_norm(parts, products, stream, scaled):
    rows, width = stream.shape
    full, count = width * len(parts), len(parts)
    patch = products[0].shape[0]
    centre = sum(p[0:1] for p in parts) / count
    squares = sum(p[1:2] + width * jnp.square(p[0:1] - centre) for p in parts)
    inverse = lax.rsqrt(squares / full + EPSILON)
    first = sum(p[2:3] for p in parts) / full
    second = inverse * sum(p[3:4] + (p[0:1] - centre) * p[2:3] for p in parts) / full
    sums = jnp.concatenate([inverse, first, second], axis=0)
    turned = jnp.concatenate([sums, centre, jnp.zeros((4, rows), F32)], axis=0).T
    normed = (stream[...] - turned[:, 3:4]) * turned[:, 0:1]
    grad = turned[:, 0:1] * (scaled[...] - turned[:, 1:2] - normed * turned[:, 2:3])
    lane, row = lanes((patch, rows)), lax.broadcasted_iota(jnp.int32, (patch, rows), 0)
    out, offset = 0.0, 0.0
    for p, product in zip(parts, products):
        slope = jnp.sum(jnp.where(lane == row, p[4:5], 0.0), axis=1, keepdims=True)
        offset += jnp.sum(jnp.where(lane == row + patch, p[4:5], 0.0), axis=1, keepdims=True)
        out += product + (p[0:1] - centre) * slope
    return normed, grad, sums, inverse * out + offset


def norm_kernel(n, *refs):
    told = [ref[...].astype(F32) for ref in refs[:n]]
    first = [t[:16] + t[16:32] + t[32:48] for t in told]
    stream_big, scaled_big, stream_guide, scaled_guide, cot = refs[n : n + 5]
    strength = refs[n + 5][refs[n + 6][0]]
    sent, grad_big, grad_guide, guided = refs[n + 7 :]
    half = 48 + (told[0].shape[0] - 48) // 2
    normed, grad, sums, out_big = model_norm(
        [f[:8] for f in first], [t[48:half] for t in told], stream_big, scaled_big
    )
    grad_big[...] = grad.astype(BF16)
    rows, width = normed.shape
    high = sums.astype(BF16).astype(F32)
    pieces = [jnp.concatenate([high, sums - high, jnp.zeros((2, rows), F32)], axis=0)]
    weighted = strength * cot[...]
    pieces += [weighted[r : r + 8] for r in range(0, weighted.shape[0], 8)]
    across = width // rows
    lines = [normed]
    for r in range(0, len(pieces), across):
        line = pieces[r : r + across]
        line += [jnp.zeros((8, width - rows * len(line)), F32)] if width > rows * len(line) else []
        lines.append(jnp.concatenate(line, axis=1))
    sent[...] = jnp.concatenate(lines, axis=0).astype(BF16)
    _, grad, _, out_guide = model_norm(
        [f[8:] for f in first], [t[half:] for t in told], stream_guide, scaled_guide
    )
    grad_guide[...] = grad.astype(BF16)
    guided[...] = out_guide + strength * (out_big - out_guide)


def whole_norm(told, streams, cot, weight):
    patch, rows = cot.shape
    width_big, width_guide = streams[0].shape[1], streams[2].shape[1]
    below = 8 * pl.cdiv(1 + patch // 8, width_big // rows)
    arrays = [*told, *streams, cot]
    return pl.pallas_call(
        functools.partial(norm_kernel, len(told)),
        in_specs=specs(arrays),
        out_shape=[
            jax.ShapeDtypeStruct((rows + below, width_big), BF16),
            jax.ShapeDtypeStruct((rows, width_big), BF16),
            jax.ShapeDtypeStruct((rows, width_guide), BF16),
            jax.ShapeDtypeStruct((patch, rows), F32),
        ],
        compiler_params=pltpu.CompilerParams(vmem_limit_bytes=VMEM_NORM),
        cost_estimate=SHORT,
        name="whole_norm",
    )(*arrays, *weight)


def shards(
    sizes,
    fc_big,
    fc_guide,
    res_big,
    res_guide,
    cotangent,
    proj_big,
    proj_guide,
    head_big,
    head_guide,
    modulation_big,
    modulation_guide,
    weight_table,
    time_index,
    weight_index,
):
    n_grp, n_seq, n_tp = sizes
    width_big, width_guide = proj_big.shape[1], proj_guide.shape[1]
    tile = 256 if width_big % 256 == 0 else 128
    width_big, width_guide = proj_big.shape[1], proj_guide.shape[1]
    tile = 256 if width_big % 256 == 0 else 128
    near_big, far_big = near_far(fc_big, n_seq)
    near_guide, far_guide = near_far(fc_guide, n_seq, near_big[1])
    early_big = project_early(near_big, proj_big, tile)
    far_big = forward(far_big, n_seq, early_big)
    big_blocks = near_big + far_big
    early_guide = project_early(after(near_guide, early_big), proj_guide, 128)
    far_guide = forward(far_guide, n_seq, (early_guide, far_big[0]))
    fc_crossed = [swap(fc_big, "grp", n_grp, g) for g in range(1, n_grp)]

    width = width_big + width_guide
    terms = project(far_big, proj_big, tile, width, early_big)
    terms = project(far_guide, proj_guide, 128, width, early_guide, terms)
    received, joined = scatter(terms, n_tp)
    begun = after((fc_crossed, modulation_big, modulation_guide), terms)
    time_late = after(time_index, terms)
    time_others = [swap(time_late, "grp", n_grp, g) for g in range(1, n_grp)]
    fc_far = [
        [block, *(swap(block, "seq", n_seq, k) for k in range(2, n_seq, 2))] for block in begun[0]
    ]
    table_big, table_guide, *tables = lookup(
        [begun[1], begun[2], *(begun[1] for _ in time_others)], [time_index, time_index, *time_others]
    )
    received, fc_far, tables, table_big, table_guide = lax.optimization_barrier(
        (received, fc_far, tables, table_big, table_guide)
    )
    fc_others = [forward(far, n_seq) for far in fc_far]
    weight = (weight_table, weight_index)

    head_big, head_guide, cot = head_big.T, head_guide.T, cotangent.T
    *streams, told = local_stats(
        received, [res_big, table_big, head_big], [res_guide, table_guide, head_guide], cot, weight
    )
    told = gather_direct(told, "seq", n_seq)
    sent, grad_big, grad_guide, guided = whole_norm(told, streams, cot, weight)

    if (n_grp, n_tp) == (2, 4):
        sent_tp, crossed = gather_pairs(sent)
        own = (big_blocks, (0, 2, 3), sent_tp, table_big)
        other = (fc_others[0], (0, 1, 2), crossed, tables[0])
        grads = contract([own, other], head_big)
        own, other = (own[0], (1,), *own[2:]), (other[0], (3,), *other[2:])
        grads = contract([own, other], head_big, grads)
    else:
        sent_tp = gather_direct(sent, "tp", n_tp)
        every = tuple(range(n_tp))
        grads = contract([(big_blocks, every, sent_tp, table_big)], head_big)
        for g in range(1, n_grp):
            crossed = [swap(x, "grp", n_grp, g) for x in sent_tp]
            sample = (fc_others[g - 1], every, crossed, tables[g - 1])
            grads = contract([sample], head_big, grads)
    return (
        guided.T,
        grads[0],
        grads[1].T,
        grad_big,
        grad_guide,
    )


def solution(mesh):
    sizes = tuple(mesh.shape[name] for name in ("grp", "seq", "tp"))
    placed = (
        P(("grp", "seq"), "tp"),
        P(("grp", "seq"), "tp"),
        P(("grp", "tp"), "seq"),
        P(("grp", "tp"), "seq"),
        P(("grp", "tp"), None),
        P("tp", "seq"),
        P("tp", "seq"),
        P("seq", None),
        P("seq", None),
        P(None, None, "seq"),
        P(None, None, "seq"),
        P(),
        P("grp"),
        P("grp"),
    )
    return jax.shard_map(
        functools.partial(shards, sizes),
        mesh=mesh,
        in_specs=placed,
        out_specs=(
            P(("grp", "tp"), None),
            P("tp", "seq"),
            P("seq", None),
            P(("grp", "tp"), "seq"),
            P(("grp", "tp"), "seq"),
        ),
        check_vma=False,
    )
```

```python
import functools

import jax
import jax.numpy as jnp
from jax import lax
from jax.experimental import pallas as pl
from jax.experimental.pallas import tpu as pltpu
from jax.sharding import PartitionSpec as P

EPSILON = 1e-06
F32 = jnp.float32
BF16 = jnp.bfloat16
VMEM = 40 * 1024 * 1024
VMEM_NORM = 24 * 1024 * 1024
VMEM_SMALL = 8 * 1024 * 1024
SHORT = pl.CostEstimate(flops=0, bytes_accessed=0, transcendentals=0)


def swap(x, axis, size, bits):
    return lax.ppermute(x, axis, [(i, i ^ bits) for i in range(size)])


def near_far(block, n, later=()):
    far = [swap(after(block, later), "seq", n, k) for k in range(2, n, 2)]
    return [block, swap(block, "seq", n, 1)], far


def forward(far, n, later=()):
    return [x for block in far for x in (block, swap(after(block, later), "seq", n, 1))]


def gather_direct(block, axis, n):
    return [block] + [swap(block, axis, n, j) for j in range(1, n)]


def after(x, *others):
    return lax.optimization_barrier((x, others))[0]


def gather_pairs(block, meanwhile):
    pairs = [(4 * g + t, 4 * (1 - g) + (t ^ 1)) for g in range(2) for t in range(4)]
    two = swap(block, "tp", 4, 2)
    across = swap(block, "grp", 2, 1)
    across_one = lax.ppermute(block, ("grp", "tp"), pairs)
    two, meanwhile = lax.optimization_barrier((across_one, across, two, meanwhile))[2:]
    three = swap(two, "tp", 4, 1)
    across_two = swap(two, "grp", 2, 1)
    three = after(three, across_two)
    across_three = swap(three, "grp", 2, 1)
    one = swap(after(block, two), "tp", 4, 1)
    return [block, one, two, three], [across, across_one, across_two, across_three], meanwhile


def add_kernel(left, right, out):
    out[...] = (left[...].astype(F32) + right[...].astype(F32)).astype(BF16)


def add(left, right):
    return pl.pallas_call(
        add_kernel,
        out_shape=jax.ShapeDtypeStruct(left.shape, BF16),
        compiler_params=pltpu.CompilerParams(vmem_limit_bytes=VMEM_SMALL),
        cost_estimate=SHORT,
        name="add",
    )(left, right)


def scatter(terms, n):
    if n != 4:
        return [terms[0]] + [swap(terms[k], "tp", n, k) for k in range(1, n)], terms[0]
    joined = add(terms[2], swap(terms[3], "tp", n, 1))
    return [terms[0], swap(terms[1], "tp", n, 1), swap(joined, "tp", n, 2)], joined


def lookup_kernel(count, *refs):
    steps, tables, outs = refs[:count], refs[count : 2 * count], refs[2 * count :]
    for step, table, out in zip(steps, tables, outs):
        for row in range(3):
            out[row : row + 1, :] = table[row, pl.ds(step[0], 1), :]


def lookup(tables, steps):
    turned = [jnp.transpose(table, (1, 0, 2)) for table in tables]
    count = len(tables)
    return pl.pallas_call(
        functools.partial(lookup_kernel, count),
        in_specs=[pl.BlockSpec(memory_space=pltpu.SMEM)] * count
        + [pl.BlockSpec(memory_space=pltpu.VMEM)] * count,
        out_shape=[jax.ShapeDtypeStruct((3, t.shape[2]), F32) for t in turned],
        compiler_params=pltpu.CompilerParams(vmem_limit_bytes=VMEM_SMALL),
        cost_estimate=SHORT,
        name="lookup",
    )(*steps, *turned)


def total(parts):
    return sum(p.astype(F32) for p in parts)


def meeting():
    return jnp.bitwise_xor(lax.axis_index("seq"), lax.axis_index("tp"))


def turned_dot(left, right):
    return lax.dot_general(left, right, (((0,), (0,)), ((), ())), preferred_element_type=F32)


def whole_block(x):
    return pl.BlockSpec(x.shape, lambda i: (0,) * x.ndim)


def project_kernel(last, filled, n, *refs):
    blocks, weight = refs[:n], refs[n]
    rows = blocks[0].shape[1]
    left = refs[-2] if last else refs[-1]

    @pl.when(pl.program_id(0) == 0)
    def _():
        for j in range(n):
            left[j * rows : (j + 1) * rows, :] = blocks[j][...].T

    product = jnp.dot(left[...], weight[...], preferred_element_type=F32).astype(BF16)
    if not last:
        refs[n + 1][...] = product
        return
    every = refs[-1]
    earlier = refs[n + 1].shape[0]
    total_blocks = n + earlier // rows
    every[:earlier, :] = refs[n + 1][...]
    every[earlier:, :] = product
    outs = refs[n + 2 + filled * total_blocks : -2]
    turn = meeting()
    for k in range(total_blocks):
        start = pl.multiple_of(jnp.bitwise_xor(turn, k) * rows, rows)
        outs[k][...] = every[pl.ds(start, rows), :]


def project_early(blocks, weight, tile):
    n = len(blocks)
    depth, columns = weight.shape
    rows = blocks[0].shape[0]
    turned = [block.T for block in blocks]
    return pl.pallas_call(
        functools.partial(project_kernel, False, False, n),
        grid=(pl.cdiv(columns, tile),),
        in_specs=[whole_block(t) for t in turned] + [pl.BlockSpec((depth, tile), lambda i: (0, i))],
        out_specs=pl.BlockSpec((n * rows, tile), lambda i: (0, i)),
        out_shape=jax.ShapeDtypeStruct((n * rows, columns), BF16),
        scratch_shapes=[pltpu.VMEM((n * rows, depth), BF16)],
        compiler_params=pltpu.CompilerParams(vmem_limit_bytes=VMEM),
        cost_estimate=SHORT,
        name="project_early",
    )(*turned, weight)


def project(blocks, weight, tile, width, early, before=()):
    n = len(blocks)
    depth, columns = weight.shape
    rows = blocks[0].shape[0]
    owners = n + early.shape[0] // rows
    turned = [block.T for block in blocks]
    first = (width - columns) // tile if before else 0
    anywhere = pl.BlockSpec(memory_space=pl.ANY)
    return pl.pallas_call(
        functools.partial(project_kernel, True, bool(before), n),
        grid=(pl.cdiv(columns, tile),),
        in_specs=[whole_block(t) for t in turned]
        + [pl.BlockSpec((depth, tile), lambda i: (0, i))]
        + [pl.BlockSpec((early.shape[0], tile), lambda i: (0, i))]
        + [anywhere] * len(before),
        out_specs=[pl.BlockSpec((rows, tile), lambda i: (0, first + i)) for _ in range(owners)],
        out_shape=[jax.ShapeDtypeStruct((rows, width), BF16) for _ in range(owners)],
        input_output_aliases={n + 2 + k: k for k in range(len(before))},
        scratch_shapes=[
            pltpu.VMEM((n * rows, depth), BF16),
            pltpu.VMEM((owners * rows, tile), BF16),
        ],
        compiler_params=pltpu.CompilerParams(vmem_limit_bytes=VMEM),
        cost_estimate=SHORT,
        name="project",
    )(*turned, weight, early, *before)


def contract_kernel(n, counts, more, *refs):
    refs = list(refs)
    take = lambda count: [refs.pop(0) for _ in range(count)]
    samples = [(take(n), take(len(slots)), *take(1)) for slots in counts]
    (head,) = take(1)
    before = take(2) if more else None
    out, head_out, signal, shelf = refs
    patch = head.shape[0]
    rows = shelf.shape[2]
    turn = meeting()

    @pl.when(pl.program_id(0) == 0)
    def _():
        gradient = before[1][...] if more else jnp.zeros(head_out.shape, F32)
        place = 0
        for _, sent, table in samples:
            gate, shift, scale = table[0:1, :], table[1:2, :], 1.0 + table[2:3, :]
            for ref in sent:
                block = ref[...].astype(F32)
                normed = block[:rows]
                pieces = [
                    block[r : r + 8, c : c + rows]
                    for r in range(rows, block.shape[0], 8)
                    for c in range(0, block.shape[1] - rows + 1, rows)
                ]
                sums = pieces[0] + jnp.concatenate([pieces[0][3:], pieces[0][:3]], axis=0)
                sums = sums.T
                cot = jnp.concatenate(pieces[1 : 1 + patch // 8], axis=0).astype(BF16)
                inverse, first, second = sums[:, 0:1], sums[:, 1:2], sums[:, 2:3]
                scaled = turned_dot(cot, head[...]) * scale
                grad = inverse * (scaled - first - normed * second)
                signal[place : place + rows, :] = (grad * gate).astype(BF16)
                shaped = (normed * scale + shift).astype(BF16)
                gradient = gradient + jnp.dot(cot, shaped, preferred_element_type=F32)
                place += rows
        head_out[...] = gradient

    left = []
    for g, (slots, (hidden, *_)) in enumerate(zip(counts, samples)):
        for j in range(n):
            shelf[g * n + j] = hidden[j][...]
        left += [shelf[g * n + jnp.bitwise_xor(turn, k)] for k in slots]
    left = jnp.concatenate(left, axis=1)
    product = jnp.dot(left, signal[...], preferred_element_type=F32)
    if more:
        product = product + before[0][...].astype(F32)
    out[...] = product.astype(BF16)


def contract(samples, head, before=None):
    n = len(samples[0][0])
    counts = [tuple(slots) for _, slots, *_ in samples]
    tokens, depth = samples[0][0][0].shape
    width = head.shape[1]
    tile = max(t for t in range(16, min(depth, 576) + 1, 16) if depth % t == 0)
    operands, in_specs = [], []
    for hidden, slots, sent, table in samples:
        operands += [block.T for block in hidden]
        in_specs += [pl.BlockSpec((tile, tokens), lambda i: (i, 0)) for _ in range(n)]
        rest = [*(sent[k] for k in slots), table]
        operands += rest
        in_specs += [whole_block(x) for x in rest]
    operands.append(head)
    in_specs.append(whole_block(head))
    if before is not None:
        operands += before
        in_specs += [pl.BlockSpec((tile, width), lambda i: (i, 0)), whole_block(before[1])]
    return pl.pallas_call(
        functools.partial(contract_kernel, n, counts, before is not None),
        grid=(depth // tile,),
        in_specs=in_specs,
        out_specs=[pl.BlockSpec((tile, width), lambda i: (i, 0)), whole_block(head)],
        out_shape=[
            jax.ShapeDtypeStruct((depth, width), BF16),
            jax.ShapeDtypeStruct(head.shape, F32),
        ],
        scratch_shapes=[
            pltpu.VMEM((sum(map(len, counts)) * tokens, width), BF16),
            pltpu.VMEM((len(samples) * n, tile, tokens), BF16),
        ],
        compiler_params=pltpu.CompilerParams(vmem_limit_bytes=VMEM),
        cost_estimate=SHORT,
        name="contract",
    )(*operands)


def lanes(shape):
    return lax.broadcasted_iota(jnp.int32, shape, 1)


def model_stats(summed, res, table, head, cot):
    patch, rows = cot.shape
    gate, shift, scale = table[0:1, :], table[1:2, :], 1.0 + table[2:3, :]
    stream = res[...].astype(F32) + gate * summed
    scaled = turned_dot(cot.astype(BF16), head[...]) * scale
    mean = jnp.mean(stream, axis=1, keepdims=True)
    centred = stream - mean
    columns = [
        mean,
        jnp.sum(centred * centred, axis=1, keepdims=True),
        jnp.sum(scaled, axis=1, keepdims=True),
        jnp.sum(scaled * centred, axis=1, keepdims=True),
    ]
    lane = lanes((rows, rows))
    spread = jnp.zeros((rows, rows), F32)
    for place, column in enumerate(columns):
        spread = jnp.where(lane == place, column, spread)
    first = spread.T[:8]
    wide = head[...].astype(F32)
    slope = jnp.sum(wide * scale, axis=1, keepdims=True)
    offset = jnp.sum(wide * shift, axis=1, keepdims=True)
    lane, row = lanes((patch, rows)), lax.broadcasted_iota(jnp.int32, (patch, rows), 0)
    both = jnp.where(lane == row, slope, jnp.where(lane == row + patch, offset, 0.0))
    both = jnp.sum(both, axis=0, keepdims=True)
    first = jnp.where(lax.broadcasted_iota(jnp.int32, (8, rows), 0) == len(columns), both, first)
    product = lax.dot_general(
        head[...], (centred * scale).astype(BF16), (((1,), (1,)), ((), ())), preferred_element_type=F32
    )
    return stream, scaled, jnp.concatenate([first, product], axis=0)


def stats_kernel(n, *refs):
    big, guide = refs[n : n + 3], refs[n + 3 : n + 6]
    cot, strength = refs[n + 6][...], refs[n + 7][refs[n + 8][0]]
    stream_big, scaled_big, stream_guide, scaled_guide, told = refs[n + 9 :]
    summed = total([ref[...] for ref in refs[:n]])
    width = big[0].shape[1]
    stream_big[...], scaled_big[...], told_big = model_stats(summed[:, :width], *big, strength * cot)
    stream_guide[...], scaled_guide[...], told_guide = model_stats(
        summed[:, width:], *guide, (1.0 - strength) * cot
    )
    left = jnp.concatenate([told_big[:8], told_guide[:8]], axis=0)
    parts = []
    for _ in range(3):
        parts.append(left.astype(BF16).astype(F32))
        left = left - parts[-1]
    told[...] = jnp.concatenate([*parts, told_big[8:], told_guide[8:]], axis=0).astype(BF16)


def specs(arrays):
    return [pl.BlockSpec(memory_space=pltpu.VMEM) for _ in arrays] + [
        pl.BlockSpec(memory_space=pltpu.SMEM) for _ in range(2)
    ]


def local_stats(received, big, guide, cot, weight):
    patch, rows = cot.shape
    widths = [model[-1].shape[1] for model in (big, guide)]
    shapes = [(rows, w) for w in widths for _ in range(2)]
    arrays = [*received, *big, *guide, cot]
    return pl.pallas_call(
        functools.partial(stats_kernel, len(received)),
        in_specs=specs(arrays),
        out_shape=[jax.ShapeDtypeStruct(shape, F32) for shape in shapes]
        + [jax.ShapeDtypeStruct((48 + 2 * patch, rows), BF16)],
        compiler_params=pltpu.CompilerParams(vmem_limit_bytes=VMEM_NORM),
        cost_estimate=SHORT,
        name="local_stats",
    )(*arrays, *weight)


def gathered(refs):
    told = [ref[...].astype(F32) for ref in refs]
    first = [t[:16] + t[16:32] + t[32:48] for t in told]
    half = 48 + (told[0].shape[0] - 48) // 2
    return (
        ([f[:8] for f in first], [t[48:half] for t in told]),
        ([f[8:] for f in first], [t[half:] for t in told]),
    )


def model_norm(parts, stream):
    rows, width = stream.shape
    full = width * len(parts)
    centre = sum(p[0:1] for p in parts) / len(parts)
    squares = sum(p[1:2] + width * jnp.square(p[0:1] - centre) for p in parts)
    inverse = lax.rsqrt(squares / full + EPSILON)
    first = sum(p[2:3] for p in parts) / full
    second = inverse * sum(p[3:4] + (p[0:1] - centre) * p[2:3] for p in parts) / full
    sums = jnp.concatenate([inverse, first, second], axis=0)
    turned = jnp.concatenate([sums, centre, jnp.zeros((4, rows), F32)], axis=0).T
    return centre, sums, turned, (stream[...] - turned[:, 3:4]) * turned[:, 0:1]


def model_rest(parts, products, stream, scaled):
    centre, sums, turned, normed = model_norm(parts, stream)
    grad = turned[:, 0:1] * (scaled[...] - turned[:, 1:2] - normed * turned[:, 2:3])
    patch, rows = products[0].shape
    lane, row = lanes((patch, rows)), lax.broadcasted_iota(jnp.int32, (patch, rows), 0)
    out, offset = 0.0, 0.0
    for p, product in zip(parts, products):
        slope = jnp.sum(jnp.where(lane == row, p[4:5], 0.0), axis=1, keepdims=True)
        offset += jnp.sum(jnp.where(lane == row + patch, p[4:5], 0.0), axis=1, keepdims=True)
        out += product + (p[0:1] - centre) * slope
    return grad.astype(BF16), sums[0:1] * out + offset


def norm_kernel(n, *refs):
    (parts, _), _ = gathered(refs[:n])
    stream, cot, weights, which, sent = refs[n:]
    _, sums, _, normed = model_norm(parts, stream)
    rows, width = normed.shape
    high = sums.astype(BF16).astype(F32)
    pieces = [jnp.concatenate([high, sums - high, jnp.zeros((2, rows), F32)], axis=0)]
    weighted = weights[which[0]] * cot[...]
    pieces += [weighted[r : r + 8] for r in range(0, weighted.shape[0], 8)]
    across = width // rows
    lines = [normed]
    for r in range(0, len(pieces), across):
        line = pieces[r : r + across]
        line += [jnp.zeros((8, width - rows * len(line)), F32)] if width > rows * len(line) else []
        lines.append(jnp.concatenate(line, axis=1))
    sent[...] = jnp.concatenate(lines, axis=0).astype(BF16)


def whole_norm(told, stream, cot, weight):
    patch, rows = cot.shape
    width = stream.shape[1]
    below = 8 * pl.cdiv(1 + patch // 8, width // rows)
    arrays = [*told, stream, cot]
    return pl.pallas_call(
        functools.partial(norm_kernel, len(told)),
        in_specs=specs(arrays),
        out_shape=jax.ShapeDtypeStruct((rows + below, width), BF16),
        compiler_params=pltpu.CompilerParams(vmem_limit_bytes=VMEM_NORM),
        cost_estimate=SHORT,
        name="whole_norm",
    )(*arrays, *weight)


def rest_kernel(n, *refs):
    big, guide = gathered(refs[:n])
    stream_big, scaled_big, stream_guide, scaled_guide, weights, which = refs[n : n + 6]
    grad_big, grad_guide, guided = refs[n + 6 :]
    grad_big[...], out_big = model_rest(*big, stream_big, scaled_big)
    grad_guide[...], out_guide = model_rest(*guide, stream_guide, scaled_guide)
    guided[...] = out_guide + weights[which[0]] * (out_big - out_guide)


def norm_rest(told, streams, patch, weight):
    rows = told[0].shape[1]
    arrays = [*told, *streams]
    return pl.pallas_call(
        functools.partial(rest_kernel, len(told)),
        in_specs=specs(arrays),
        out_shape=[
            jax.ShapeDtypeStruct(streams[0].shape, BF16),
            jax.ShapeDtypeStruct(streams[2].shape, BF16),
            jax.ShapeDtypeStruct((patch, rows), F32),
        ],
        compiler_params=pltpu.CompilerParams(vmem_limit_bytes=VMEM_NORM),
        cost_estimate=SHORT,
        name="norm_rest",
    )(*arrays, *weight)


def shards(
    sizes,
    fc_big,
    fc_guide,
    res_big,
    res_guide,
    cotangent,
    proj_big,
    proj_guide,
    head_big,
    head_guide,
    modulation_big,
    modulation_guide,
    weight_table,
    time_index,
    weight_index,
):
    n_grp, n_seq, n_tp = sizes
    width_big, width_guide = proj_big.shape[1], proj_guide.shape[1]
    tile = 256 if width_big % 256 == 0 else 128
    width_big, width_guide = proj_big.shape[1], proj_guide.shape[1]
    tile = 256 if width_big % 256 == 0 else 128
    near_big, far_big = near_far(fc_big, n_seq)
    near_guide, far_guide = near_far(fc_guide, n_seq, near_big[1])
    early_big = project_early(near_big, proj_big, tile)
    far_big = forward(far_big, n_seq, early_big)
    big_blocks = near_big + far_big
    early_guide = project_early(after(near_guide, early_big), proj_guide, 128)
    far_guide = forward(far_guide, n_seq, (early_guide, far_big[0]))

    width = width_big + width_guide
    terms = project(far_big, proj_big, tile, width, early_big)
    fc_late = after(fc_big, terms)
    fc_crossed = [swap(fc_late, "grp", n_grp, g) for g in range(1, n_grp)]
    terms = project(far_guide, proj_guide, 128, width, early_guide, terms)
    received, joined = scatter(terms, n_tp)
    begun = after((fc_crossed, modulation_big, modulation_guide), terms)
    time_late = after(time_index, terms)
    time_others = [swap(time_late, "grp", n_grp, g) for g in range(1, n_grp)]
    fc_far = [
        [block, *(swap(block, "seq", n_seq, k) for k in range(2, n_seq, 2))] for block in begun[0]
    ]
    table_big, table_guide, *tables = lookup(
        [begun[1], begun[2], *(begun[1] for _ in time_others)], [time_index, time_index, *time_others]
    )
    received, fc_far, tables, table_big, table_guide = lax.optimization_barrier(
        (received, fc_far, tables, table_big, table_guide)
    )
    fc_others = [forward(far, n_seq) for far in fc_far]
    weight = (weight_table, weight_index)

    head_big, head_guide, cot = head_big.T, head_guide.T, cotangent.T
    *streams, told = local_stats(
        received, [res_big, table_big, head_big], [res_guide, table_guide, head_guide], cot, weight
    )
    told = gather_direct(told, "seq", n_seq)
    sent = whole_norm(told, streams[0], cot, weight)
    rest = norm_rest(told, streams, cot.shape[0], weight)

    if (n_grp, n_tp) == (2, 4):
        sent_tp, crossed, rest = gather_pairs(sent, rest)
        own = (big_blocks, (0, 2, 3), sent_tp, table_big)
        other = (fc_others[0], (0, 1, 2), crossed, tables[0])
        grads = contract([own, other], head_big)
        own, other = (own[0], (1,), *own[2:]), (other[0], (3,), *other[2:])
        grads = contract([own, other], head_big, grads)
    else:
        sent_tp = gather_direct(sent, "tp", n_tp)
        every = tuple(range(n_tp))
        grads = contract([(big_blocks, every, sent_tp, table_big)], head_big)
        for g in range(1, n_grp):
            crossed = [swap(x, "grp", n_grp, g) for x in sent_tp]
            sample = (fc_others[g - 1], every, crossed, tables[g - 1])
            grads = contract([sample], head_big, grads)
    return (
        rest[2].T,
        grads[0],
        grads[1].T,
        rest[0],
        rest[1],
    )


def solution(mesh):
    sizes = tuple(mesh.shape[name] for name in ("grp", "seq", "tp"))
    placed = (
        P(("grp", "seq"), "tp"),
        P(("grp", "seq"), "tp"),
        P(("grp", "tp"), "seq"),
        P(("grp", "tp"), "seq"),
        P(("grp", "tp"), None),
        P("tp", "seq"),
        P("tp", "seq"),
        P("seq", None),
        P("seq", None),
        P(None, None, "seq"),
        P(None, None, "seq"),
        P(),
        P("grp"),
        P("grp"),
    )
    return jax.shard_map(
        functools.partial(shards, sizes),
        mesh=mesh,
        in_specs=placed,
        out_specs=(
            P(("grp", "tp"), None),
            P("tp", "seq"),
            P("seq", None),
            P(("grp", "tp"), "seq"),
            P(("grp", "tp"), "seq"),
        ),
        check_vma=False,
    )
```

```python
import functools

import jax
import jax.numpy as jnp
from jax import lax
from jax.experimental import pallas as pl
from jax.experimental.pallas import tpu as pltpu
from jax.sharding import PartitionSpec as P

EPSILON = 1e-06
F32 = jnp.float32
BF16 = jnp.bfloat16
VMEM = 40 * 1024 * 1024
VMEM_NORM = 24 * 1024 * 1024
VMEM_SMALL = 8 * 1024 * 1024
SHORT = pl.CostEstimate(flops=0, bytes_accessed=0, transcendentals=0)


def swap(x, axis, size, bits):
    return lax.ppermute(x, axis, [(i, i ^ bits) for i in range(size)])


def near_far(block, n, later=()):
    far = [swap(after(block, later), "seq", n, k) for k in range(2, n, 2)]
    return [block, swap(block, "seq", n, 1)], far


def forward(far, n, later=()):
    return [x for block in far for x in (block, swap(after(block, later), "seq", n, 1))]


def gather_direct(block, axis, n):
    return [block] + [swap(block, axis, n, j) for j in range(1, n)]


def after(x, *others):
    return lax.optimization_barrier((x, others))[0]


def gather_pairs(block, meanwhile):
    pairs = [(4 * g + t, 4 * (1 - g) + (t ^ 1)) for g in range(2) for t in range(4)]
    two = swap(block, "tp", 4, 2)
    across = swap(block, "grp", 2, 1)
    across_one = lax.ppermute(block, ("grp", "tp"), pairs)
    two, meanwhile = lax.optimization_barrier((across, across_one, two, meanwhile))[2:]
    three = swap(two, "tp", 4, 1)
    across_two = swap(two, "grp", 2, 1)
    three = after(three, across_two)
    across_three = swap(three, "grp", 2, 1)
    one = swap(after(block, two), "tp", 4, 1)
    return [block, one, two, three], [across, across_one, across_two, across_three], meanwhile


def add_kernel(left, right, out):
    out[...] = (left[...].astype(F32) + right[...].astype(F32)).astype(BF16)


def add(left, right):
    return pl.pallas_call(
        add_kernel,
        out_shape=jax.ShapeDtypeStruct(left.shape, BF16),
        compiler_params=pltpu.CompilerParams(vmem_limit_bytes=VMEM_SMALL),
        cost_estimate=SHORT,
        name="add",
    )(left, right)


def scatter(terms, n):
    if n != 4:
        return [terms[0]] + [swap(terms[k], "tp", n, k) for k in range(1, n)], terms[0]
    joined = add(terms[2], swap(terms[3], "tp", n, 1))
    return [terms[0], swap(terms[1], "tp", n, 1), swap(joined, "tp", n, 2)], joined


def lookup_kernel(count, *refs):
    steps, tables, outs = refs[:count], refs[count : 2 * count], refs[2 * count :]
    for step, table, out in zip(steps, tables, outs):
        for row in range(3):
            out[row : row + 1, :] = table[row, pl.ds(step[0], 1), :]


def lookup(tables, steps):
    turned = [jnp.transpose(table, (1, 0, 2)) for table in tables]
    count = len(tables)
    return pl.pallas_call(
        functools.partial(lookup_kernel, count),
        in_specs=[pl.BlockSpec(memory_space=pltpu.SMEM)] * count
        + [pl.BlockSpec(memory_space=pltpu.VMEM)] * count,
        out_shape=[jax.ShapeDtypeStruct((3, t.shape[2]), F32) for t in turned],
        compiler_params=pltpu.CompilerParams(vmem_limit_bytes=VMEM_SMALL),
        cost_estimate=SHORT,
        name="lookup",
    )(*steps, *turned)


def total(parts):
    return sum(p.astype(F32) for p in parts)


def meeting():
    return jnp.bitwise_xor(lax.axis_index("seq"), lax.axis_index("tp"))


def turned_dot(left, right):
    return lax.dot_general(left, right, (((0,), (0,)), ((), ())), preferred_element_type=F32)


def whole_block(x):
    return pl.BlockSpec(x.shape, lambda i: (0,) * x.ndim)


def in_place():
    return pl.BlockSpec(memory_space=pltpu.VMEM)


def weight_spec(weight, tile):
    if weight.shape[1] % tile:
        return pl.BlockSpec((weight.shape[0], tile), lambda i: (0, i))
    return in_place()


def project_kernel(last, filled, n, *refs):
    blocks, weight = refs[:n], refs[n]
    rows = blocks[0].shape[1]
    left = refs[-2] if last else refs[-1]

    @pl.when(pl.program_id(0) == 0)
    def _():
        for j in range(n):
            left[j * rows : (j + 1) * rows, :] = blocks[j][...].T

    tile = refs[n + 1].shape[1]
    if weight.shape[1] > tile:
        here = pl.ds(pl.multiple_of(pl.program_id(0) * tile, tile), tile)
        product = jnp.dot(left[...], weight[:, here], preferred_element_type=F32).astype(BF16)
    else:
        product = jnp.dot(left[...], weight[...], preferred_element_type=F32).astype(BF16)
    if not last:
        refs[n + 1][...] = product
        return
    every = refs[-1]
    earlier = refs[n + 1].shape[0]
    total_blocks = n + earlier // rows
    every[:earlier, :] = refs[n + 1][...]
    every[earlier:, :] = product
    outs = refs[n + 2 + filled * total_blocks : -2]
    turn = meeting()
    for k in range(total_blocks):
        start = pl.multiple_of(jnp.bitwise_xor(turn, k) * rows, rows)
        outs[k][...] = every[pl.ds(start, rows), :]


def project_early(blocks, weight, tile):
    n = len(blocks)
    depth, columns = weight.shape
    rows = blocks[0].shape[0]
    turned = [block.T for block in blocks]
    return pl.pallas_call(
        functools.partial(project_kernel, False, False, n),
        grid=(pl.cdiv(columns, tile),),
        in_specs=[in_place() for _ in turned] + [weight_spec(weight, tile)],
        out_specs=pl.BlockSpec((n * rows, tile), lambda i: (0, i)),
        out_shape=jax.ShapeDtypeStruct((n * rows, columns), BF16),
        scratch_shapes=[pltpu.VMEM((n * rows, depth), BF16)],
        compiler_params=pltpu.CompilerParams(vmem_limit_bytes=VMEM),
        cost_estimate=SHORT,
        name="project_early",
    )(*turned, weight)


def project(blocks, weight, tile, width, early, before=()):
    n = len(blocks)
    depth, columns = weight.shape
    rows = blocks[0].shape[0]
    owners = n + early.shape[0] // rows
    turned = [block.T for block in blocks]
    first = (width - columns) // tile if before else 0
    anywhere = pl.BlockSpec(memory_space=pl.ANY)
    return pl.pallas_call(
        functools.partial(project_kernel, True, bool(before), n),
        grid=(pl.cdiv(columns, tile),),
        in_specs=[in_place() for _ in turned]
        + [weight_spec(weight, tile)]
        + [pl.BlockSpec((early.shape[0], tile), lambda i: (0, i))]
        + [anywhere] * len(before),
        out_specs=[pl.BlockSpec((rows, tile), lambda i: (0, first + i)) for _ in range(owners)],
        out_shape=[jax.ShapeDtypeStruct((rows, width), BF16) for _ in range(owners)],
        input_output_aliases={n + 2 + k: k for k in range(len(before))},
        scratch_shapes=[
            pltpu.VMEM((n * rows, depth), BF16),
            pltpu.VMEM((owners * rows, tile), BF16),
        ],
        compiler_params=pltpu.CompilerParams(vmem_limit_bytes=VMEM),
        cost_estimate=SHORT,
        name="project",
    )(*turned, weight, early, *before)


def contract_kernel(n, counts, more, *refs):
    refs = list(refs)
    take = lambda count: [refs.pop(0) for _ in range(count)]
    samples = [(take(n), take(len(slots)), *take(1)) for slots in counts]
    (head,) = take(1)
    before = take(2) if more else None
    out, head_out, signal, shelf = refs
    patch = head.shape[0]
    rows = shelf.shape[2]
    turn = meeting()

    @pl.when(pl.program_id(0) == 0)
    def _():
        gradient = before[1][...] if more else jnp.zeros(head_out.shape, F32)
        place = 0
        for _, sent, table in samples:
            gate, shift, scale = table[0:1, :], table[1:2, :], 1.0 + table[2:3, :]
            for ref in sent:
                block = ref[...].astype(F32)
                normed = block[:rows]
                pieces = [
                    block[r : r + 8, c : c + rows]
                    for r in range(rows, block.shape[0], 8)
                    for c in range(0, block.shape[1] - rows + 1, rows)
                ]
                sums = pieces[0] + jnp.concatenate([pieces[0][3:], pieces[0][:3]], axis=0)
                sums = sums.T
                cot = jnp.concatenate(pieces[1 : 1 + patch // 8], axis=0).astype(BF16)
                inverse, first, second = sums[:, 0:1], sums[:, 1:2], sums[:, 2:3]
                scaled = turned_dot(cot, head[...]) * scale
                grad = inverse * (scaled - first - normed * second)
                signal[place : place + rows, :] = (grad * gate).astype(BF16)
                shaped = (normed * scale + shift).astype(BF16)
                gradient = gradient + jnp.dot(cot, shaped, preferred_element_type=F32)
                place += rows
        head_out[...] = gradient

    tile = out.shape[0]
    here = pl.ds(pl.multiple_of(pl.program_id(0) * tile, tile), tile)
    wanted = [(hidden, k) for slots, (hidden, *_) in zip(counts, samples) for k in slots]
    for place, (hidden, k) in enumerate(wanted):
        for j in range(n):

            @pl.when(jnp.bitwise_xor(turn, k) == j)
            def _():
                shelf[place] = hidden[j][here, :]

    left = jnp.concatenate([shelf[place] for place in range(len(wanted))], axis=1)
    product = jnp.dot(left, signal[...], preferred_element_type=F32)
    if more:
        product = product + before[0][here, :].astype(F32)
    out[...] = product.astype(BF16)


def contract(samples, head, before=None):
    n = len(samples[0][0])
    counts = [tuple(slots) for _, slots, *_ in samples]
    tokens, depth = samples[0][0][0].shape
    width = head.shape[1]
    tile = max(t for t in range(16, min(depth, 576) + 1, 16) if depth % t == 0)
    operands, in_specs = [], []
    for hidden, slots, sent, table in samples:
        operands += [block.T for block in hidden]
        in_specs += [in_place() for _ in range(n)]
        rest = [*(sent[k] for k in slots), table]
        operands += rest
        in_specs += [whole_block(x) for x in rest]
    operands.append(head)
    in_specs.append(whole_block(head))
    if before is not None:
        operands += before
        in_specs += [in_place(), whole_block(before[1])]
    return pl.pallas_call(
        functools.partial(contract_kernel, n, counts, before is not None),
        grid=(depth // tile,),
        in_specs=in_specs,
        out_specs=[pl.BlockSpec((tile, width), lambda i: (i, 0)), whole_block(head)],
        out_shape=[
            jax.ShapeDtypeStruct((depth, width), BF16),
            jax.ShapeDtypeStruct(head.shape, F32),
        ],
        scratch_shapes=[
            pltpu.VMEM((sum(map(len, counts)) * tokens, width), BF16),
            pltpu.VMEM((sum(map(len, counts)), tile, tokens), BF16),
        ],
        compiler_params=pltpu.CompilerParams(vmem_limit_bytes=VMEM),
        cost_estimate=SHORT,
        name="contract",
    )(*operands)


def lanes(shape):
    return lax.broadcasted_iota(jnp.int32, shape, 1)


def model_stats(summed, res, table, head, cot):
    patch, rows = cot.shape
    gate, shift, scale = table[0:1, :], table[1:2, :], 1.0 + table[2:3, :]
    stream = res[...].astype(F32) + gate * summed
    scaled = turned_dot(cot.astype(BF16), head[...]) * scale
    mean = jnp.mean(stream, axis=1, keepdims=True)
    centred = stream - mean
    columns = [
        mean,
        jnp.sum(centred * centred, axis=1, keepdims=True),
        jnp.sum(scaled, axis=1, keepdims=True),
        jnp.sum(scaled * centred, axis=1, keepdims=True),
    ]
    lane = lanes((rows, rows))
    spread = jnp.zeros((rows, rows), F32)
    for place, column in enumerate(columns):
        spread = jnp.where(lane == place, column, spread)
    first = spread.T[:8]
    wide = head[...].astype(F32)
    slope = jnp.sum(wide * scale, axis=1, keepdims=True)
    offset = jnp.sum(wide * shift, axis=1, keepdims=True)
    lane, row = lanes((patch, rows)), lax.broadcasted_iota(jnp.int32, (patch, rows), 0)
    both = jnp.where(lane == row, slope, jnp.where(lane == row + patch, offset, 0.0))
    both = jnp.sum(both, axis=0, keepdims=True)
    first = jnp.where(lax.broadcasted_iota(jnp.int32, (8, rows), 0) == len(columns), both, first)
    product = lax.dot_general(
        head[...], (centred * scale).astype(BF16), (((1,), (1,)), ((), ())), preferred_element_type=F32
    )
    return stream, scaled, jnp.concatenate([first, product], axis=0)


def stats_kernel(n, *refs):
    big, guide = refs[n : n + 3], refs[n + 3 : n + 6]
    cot, strength = refs[n + 6][...], refs[n + 7][refs[n + 8][0]]
    stream_big, scaled_big, stream_guide, scaled_guide, told = refs[n + 9 :]
    summed = total([ref[...] for ref in refs[:n]])
    width = big[0].shape[1]
    stream_big[...], scaled_big[...], told_big = model_stats(summed[:, :width], *big, strength * cot)
    stream_guide[...], scaled_guide[...], told_guide = model_stats(
        summed[:, width:], *guide, (1.0 - strength) * cot
    )
    left = jnp.concatenate([told_big[:8], told_guide[:8]], axis=0)
    parts = []
    for _ in range(3):
        parts.append(left.astype(BF16).astype(F32))
        left = left - parts[-1]
    told[...] = jnp.concatenate([*parts, told_big[8:], told_guide[8:]], axis=0).astype(BF16)


def specs(arrays):
    return [pl.BlockSpec(memory_space=pltpu.VMEM) for _ in arrays] + [
        pl.BlockSpec(memory_space=pltpu.SMEM) for _ in range(2)
    ]


def local_stats(received, big, guide, cot, weight):
    patch, rows = cot.shape
    widths = [model[-1].shape[1] for model in (big, guide)]
    shapes = [(rows, w) for w in widths for _ in range(2)]
    arrays = [*received, *big, *guide, cot]
    return pl.pallas_call(
        functools.partial(stats_kernel, len(received)),
        in_specs=specs(arrays),
        out_shape=[jax.ShapeDtypeStruct(shape, F32) for shape in shapes]
        + [jax.ShapeDtypeStruct((48 + 2 * patch, rows), BF16)],
        compiler_params=pltpu.CompilerParams(vmem_limit_bytes=VMEM_NORM),
        cost_estimate=SHORT,
        name="local_stats",
    )(*arrays, *weight)


def gathered(refs):
    told = [ref[...].astype(F32) for ref in refs]
    first = [t[:16] + t[16:32] + t[32:48] for t in told]
    half = 48 + (told[0].shape[0] - 48) // 2
    return (
        ([f[:8] for f in first], [t[48:half] for t in told]),
        ([f[8:] for f in first], [t[half:] for t in told]),
    )


def model_norm(parts, stream):
    rows, width = stream.shape
    full = width * len(parts)
    centre = sum(p[0:1] for p in parts) / len(parts)
    squares = sum(p[1:2] + width * jnp.square(p[0:1] - centre) for p in parts)
    inverse = lax.rsqrt(squares / full + EPSILON)
    first = sum(p[2:3] for p in parts) / full
    second = inverse * sum(p[3:4] + (p[0:1] - centre) * p[2:3] for p in parts) / full
    sums = jnp.concatenate([inverse, first, second], axis=0)
    turned = jnp.concatenate([sums, centre, jnp.zeros((4, rows), F32)], axis=0).T
    return centre, sums, turned, (stream[...] - turned[:, 3:4]) * turned[:, 0:1]


def model_rest(parts, products, stream, scaled):
    centre, sums, turned, normed = model_norm(parts, stream)
    grad = turned[:, 0:1] * (scaled[...] - turned[:, 1:2] - normed * turned[:, 2:3])
    patch, rows = products[0].shape
    lane, row = lanes((patch, rows)), lax.broadcasted_iota(jnp.int32, (patch, rows), 0)
    out, offset = 0.0, 0.0
    for p, product in zip(parts, products):
        slope = jnp.sum(jnp.where(lane == row, p[4:5], 0.0), axis=1, keepdims=True)
        offset += jnp.sum(jnp.where(lane == row + patch, p[4:5], 0.0), axis=1, keepdims=True)
        out += product + (p[0:1] - centre) * slope
    return grad.astype(BF16), sums[0:1] * out + offset


def norm_kernel(n, *refs):
    (parts, _), _ = gathered(refs[:n])
    stream, cot, weights, which, sent = refs[n:]
    _, sums, _, normed = model_norm(parts, stream)
    rows, width = normed.shape
    high = sums.astype(BF16).astype(F32)
    pieces = [jnp.concatenate([high, sums - high, jnp.zeros((2, rows), F32)], axis=0)]
    weighted = weights[which[0]] * cot[...]
    pieces += [weighted[r : r + 8] for r in range(0, weighted.shape[0], 8)]
    across = width // rows
    lines = [normed]
    for r in range(0, len(pieces), across):
        line = pieces[r : r + across]
        line += [jnp.zeros((8, width - rows * len(line)), F32)] if width > rows * len(line) else []
        lines.append(jnp.concatenate(line, axis=1))
    sent[...] = jnp.concatenate(lines, axis=0).astype(BF16)


def whole_norm(told, stream, cot, weight):
    patch, rows = cot.shape
    width = stream.shape[1]
    below = 8 * pl.cdiv(1 + patch // 8, width // rows)
    arrays = [*told, stream, cot]
    return pl.pallas_call(
        functools.partial(norm_kernel, len(told)),
        in_specs=specs(arrays),
        out_shape=jax.ShapeDtypeStruct((rows + below, width), BF16),
        compiler_params=pltpu.CompilerParams(vmem_limit_bytes=VMEM_NORM),
        cost_estimate=SHORT,
        name="whole_norm",
    )(*arrays, *weight)


def rest_kernel(n, *refs):
    big, guide = gathered(refs[:n])
    stream_big, scaled_big, stream_guide, scaled_guide, weights, which = refs[n : n + 6]
    grad_big, grad_guide, guided = refs[n + 6 :]
    grad_big[...], out_big = model_rest(*big, stream_big, scaled_big)
    grad_guide[...], out_guide = model_rest(*guide, stream_guide, scaled_guide)
    guided[...] = out_guide + weights[which[0]] * (out_big - out_guide)


def norm_rest(told, streams, patch, weight):
    rows = told[0].shape[1]
    arrays = [*told, *streams]
    return pl.pallas_call(
        functools.partial(rest_kernel, len(told)),
        in_specs=specs(arrays),
        out_shape=[
            jax.ShapeDtypeStruct(streams[0].shape, BF16),
            jax.ShapeDtypeStruct(streams[2].shape, BF16),
            jax.ShapeDtypeStruct((patch, rows), F32),
        ],
        compiler_params=pltpu.CompilerParams(vmem_limit_bytes=VMEM_NORM),
        cost_estimate=SHORT,
        name="norm_rest",
    )(*arrays, *weight)


def shards(
    sizes,
    fc_big,
    fc_guide,
    res_big,
    res_guide,
    cotangent,
    proj_big,
    proj_guide,
    head_big,
    head_guide,
    modulation_big,
    modulation_guide,
    weight_table,
    time_index,
    weight_index,
):
    n_grp, n_seq, n_tp = sizes
    width_big, width_guide = proj_big.shape[1], proj_guide.shape[1]
    tile = next(t for t in (640, 256, 128) if width_big % t == 0)
    width_big, width_guide = proj_big.shape[1], proj_guide.shape[1]
    tile = next(t for t in (640, 256, 128) if width_big % t == 0)
    near_big, far_big = near_far(fc_big, n_seq)
    near_guide, far_guide = near_far(fc_guide, n_seq, near_big[1])
    early_big = project_early(near_big, proj_big, tile)
    far_big = forward(far_big, n_seq, early_big)
    big_blocks = near_big + far_big
    early_guide = project_early(after(near_guide, early_big), proj_guide, 128)
    fc_crossed = [swap(fc_big, "grp", n_grp, g) for g in range(1, n_grp)]
    far_guide = forward(far_guide, n_seq, (early_guide, far_big[0], fc_crossed))

    width = width_big + width_guide
    terms = project(far_big, proj_big, tile, width, early_big)
    terms = project(far_guide, proj_guide, 128, width, early_guide, terms)
    received, joined = scatter(terms, n_tp)
    begun = after((fc_crossed, modulation_big, modulation_guide), terms)
    time_late = after(time_index, terms)
    time_others = [swap(time_late, "grp", n_grp, g) for g in range(1, n_grp)]
    fc_far = [
        [block, *(swap(block, "seq", n_seq, k) for k in range(2, n_seq, 2))] for block in begun[0]
    ]
    table_big, table_guide, *tables = lookup(
        [begun[1], begun[2], *(begun[1] for _ in time_others)], [time_index, time_index, *time_others]
    )
    received, fc_far, tables, table_big, table_guide = lax.optimization_barrier(
        (received, fc_far, tables, table_big, table_guide)
    )
    fc_others = [forward(far, n_seq) for far in fc_far]
    weight = (weight_table, weight_index)

    head_big, head_guide, cot = head_big.T, head_guide.T, cotangent.T
    *streams, told = local_stats(
        received, [res_big, table_big, head_big], [res_guide, table_guide, head_guide], cot, weight
    )
    told = gather_direct(told, "seq", n_seq)
    sent = whole_norm(told, streams[0], cot, weight)
    rest = norm_rest(told, streams, cot.shape[0], weight)

    if (n_grp, n_tp) == (2, 4):
        sent_tp, crossed, rest = gather_pairs(sent, rest)
        own = (big_blocks, (0, 2, 3), sent_tp, table_big)
        other = (fc_others[0], (0, 1, 2), crossed, tables[0])
        grads = contract([own, other], head_big)
        own, other = (own[0], (1,), *own[2:]), (other[0], (3,), *other[2:])
        grads = contract([own, other], head_big, grads)
    else:
        sent_tp = gather_direct(sent, "tp", n_tp)
        every = tuple(range(n_tp))
        grads = contract([(big_blocks, every, sent_tp, table_big)], head_big)
        for g in range(1, n_grp):
            crossed = [swap(x, "grp", n_grp, g) for x in sent_tp]
            sample = (fc_others[g - 1], every, crossed, tables[g - 1])
            grads = contract([sample], head_big, grads)
    return (
        rest[2].T,
        grads[0],
        grads[1].T,
        rest[0],
        rest[1],
    )


def solution(mesh):
    sizes = tuple(mesh.shape[name] for name in ("grp", "seq", "tp"))
    placed = (
        P(("grp", "seq"), "tp"),
        P(("grp", "seq"), "tp"),
        P(("grp", "tp"), "seq"),
        P(("grp", "tp"), "seq"),
        P(("grp", "tp"), None),
        P("tp", "seq"),
        P("tp", "seq"),
        P("seq", None),
        P("seq", None),
        P(None, None, "seq"),
        P(None, None, "seq"),
        P(),
        P("grp"),
        P("grp"),
    )
    return jax.shard_map(
        functools.partial(shards, sizes),
        mesh=mesh,
        in_specs=placed,
        out_specs=(
            P(("grp", "tp"), None),
            P("tp", "seq"),
            P("seq", None),
            P(("grp", "tp"), "seq"),
            P(("grp", "tp"), "seq"),
        ),
        check_vma=False,
    )
```

```python
import functools

import jax
import jax.numpy as jnp
from jax import lax
from jax.experimental import pallas as pl
from jax.experimental.pallas import tpu as pltpu
from jax.sharding import PartitionSpec as P

EPSILON = 1e-06
F32 = jnp.float32
BF16 = jnp.bfloat16
VMEM = 40 * 1024 * 1024
VMEM_NORM = 24 * 1024 * 1024
VMEM_SMALL = 8 * 1024 * 1024
SHORT = pl.CostEstimate(flops=0, bytes_accessed=0, transcendentals=0)


def swap(x, axis, size, bits):
    return lax.ppermute(x, axis, [(i, i ^ bits) for i in range(size)])


def near_far(block, n, later=()):
    far = [swap(after(block, later), "seq", n, k) for k in range(2, n, 2)]
    return [block, swap(block, "seq", n, 1)], far


def forward(far, n, later=()):
    return [x for block in far for x in (block, swap(after(block, later), "seq", n, 1))]


def gather_direct(block, axis, n):
    return [block] + [swap(block, axis, n, j) for j in range(1, n)]


def after(x, *others):
    return lax.optimization_barrier((x, others))[0]


def gather_pairs(block, meanwhile):
    pairs = [(4 * g + t, 4 * (1 - g) + (t ^ 1)) for g in range(2) for t in range(4)]
    two = swap(block, "tp", 4, 2)
    across = swap(block, "grp", 2, 1)
    across_one = lax.ppermute(block, ("grp", "tp"), pairs)
    two, meanwhile = lax.optimization_barrier((across, across_one, two, meanwhile))[2:]
    three = swap(two, "tp", 4, 1)
    across_two = swap(two, "grp", 2, 1)
    three = after(three, across_two)
    across_three = swap(three, "grp", 2, 1)
    one = swap(after(block, three), "tp", 4, 1)
    return [block, one, two, three], [across, across_one, across_two, across_three], meanwhile


def add_kernel(left, right, out):
    out[...] = (left[...].astype(F32) + right[...].astype(F32)).astype(BF16)


def add(left, right):
    return pl.pallas_call(
        add_kernel,
        out_shape=jax.ShapeDtypeStruct(left.shape, BF16),
        compiler_params=pltpu.CompilerParams(vmem_limit_bytes=VMEM_SMALL),
        cost_estimate=SHORT,
        name="add",
    )(left, right)


def scatter(terms, n):
    if n != 4:
        return [terms[0]] + [swap(terms[k], "tp", n, k) for k in range(1, n)], terms[0]
    joined = add(terms[2], swap(terms[3], "tp", n, 1))
    return [terms[0], swap(terms[1], "tp", n, 1), swap(joined, "tp", n, 2)], joined


def lookup_kernel(count, *refs):
    steps, tables, outs = refs[:count], refs[count : 2 * count], refs[2 * count :]
    for step, table, out in zip(steps, tables, outs):
        for row in range(3):
            out[row : row + 1, :] = table[row, pl.ds(step[0], 1), :]


def lookup(tables, steps):
    turned = [jnp.transpose(table, (1, 0, 2)) for table in tables]
    count = len(tables)
    return pl.pallas_call(
        functools.partial(lookup_kernel, count),
        in_specs=[pl.BlockSpec(memory_space=pltpu.SMEM)] * count
        + [pl.BlockSpec(memory_space=pltpu.VMEM)] * count,
        out_shape=[jax.ShapeDtypeStruct((3, t.shape[2]), F32) for t in turned],
        compiler_params=pltpu.CompilerParams(vmem_limit_bytes=VMEM_SMALL),
        cost_estimate=SHORT,
        name="lookup",
    )(*steps, *turned)


def total(parts):
    return sum(p.astype(F32) for p in parts)


def meeting():
    return jnp.bitwise_xor(lax.axis_index("seq"), lax.axis_index("tp"))


def turned_dot(left, right):
    return lax.dot_general(left, right, (((0,), (0,)), ((), ())), preferred_element_type=F32)


def whole_block(x):
    return pl.BlockSpec(x.shape, lambda i: (0,) * x.ndim)


def in_place():
    return pl.BlockSpec(memory_space=pltpu.VMEM)


def weight_spec(weight, tile):
    if weight.shape[1] % tile:
        return pl.BlockSpec((weight.shape[0], tile), lambda i: (0, i))
    return in_place()


def project_kernel(last, filled, n, *refs):
    blocks, weight = refs[:n], refs[n]
    rows = blocks[0].shape[1]
    left = refs[-2] if last else refs[-1]

    @pl.when(pl.program_id(0) == 0)
    def _():
        for j in range(n):
            left[j * rows : (j + 1) * rows, :] = blocks[j][...].T

    tile = refs[n + 1].shape[1]
    if weight.shape[1] > tile:
        here = pl.ds(pl.multiple_of(pl.program_id(0) * tile, tile), tile)
        product = jnp.dot(left[...], weight[:, here], preferred_element_type=F32).astype(BF16)
    else:
        product = jnp.dot(left[...], weight[...], preferred_element_type=F32).astype(BF16)
    if not last:
        refs[n + 1][...] = product
        return
    every = refs[-1]
    earlier = refs[n + 1].shape[0]
    total_blocks = n + earlier // rows
    every[:earlier, :] = refs[n + 1][...]
    every[earlier:, :] = product
    outs = refs[n + 2 + filled * total_blocks : -2]
    turn = meeting()
    for k in range(total_blocks):
        start = pl.multiple_of(jnp.bitwise_xor(turn, k) * rows, rows)
        outs[k][...] = every[pl.ds(start, rows), :]


def project_early(blocks, weight, tile):
    n = len(blocks)
    depth, columns = weight.shape
    rows = blocks[0].shape[0]
    turned = [block.T for block in blocks]
    return pl.pallas_call(
        functools.partial(project_kernel, False, False, n),
        grid=(pl.cdiv(columns, tile),),
        in_specs=[in_place() for _ in turned] + [weight_spec(weight, tile)],
        out_specs=pl.BlockSpec((n * rows, tile), lambda i: (0, i)),
        out_shape=jax.ShapeDtypeStruct((n * rows, columns), BF16),
        scratch_shapes=[pltpu.VMEM((n * rows, depth), BF16)],
        compiler_params=pltpu.CompilerParams(vmem_limit_bytes=VMEM),
        cost_estimate=SHORT,
        name="project_early",
    )(*turned, weight)


def project(blocks, weight, tile, width, early, before=()):
    n = len(blocks)
    depth, columns = weight.shape
    rows = blocks[0].shape[0]
    owners = n + early.shape[0] // rows
    turned = [block.T for block in blocks]
    first = (width - columns) // tile if before else 0
    anywhere = pl.BlockSpec(memory_space=pl.ANY)
    return pl.pallas_call(
        functools.partial(project_kernel, True, bool(before), n),
        grid=(pl.cdiv(columns, tile),),
        in_specs=[in_place() for _ in turned]
        + [weight_spec(weight, tile)]
        + [pl.BlockSpec((early.shape[0], tile), lambda i: (0, i))]
        + [anywhere] * len(before),
        out_specs=[pl.BlockSpec((rows, tile), lambda i: (0, first + i)) for _ in range(owners)],
        out_shape=[jax.ShapeDtypeStruct((rows, width), BF16) for _ in range(owners)],
        input_output_aliases={n + 2 + k: k for k in range(len(before))},
        scratch_shapes=[
            pltpu.VMEM((n * rows, depth), BF16),
            pltpu.VMEM((owners * rows, tile), BF16),
        ],
        compiler_params=pltpu.CompilerParams(vmem_limit_bytes=VMEM),
        cost_estimate=SHORT,
        name="project",
    )(*turned, weight, early, *before)


def contract_kernel(n, counts, more, *refs):
    refs = list(refs)
    take = lambda count: [refs.pop(0) for _ in range(count)]
    samples = [(take(n), take(len(slots)), *take(1)) for slots in counts]
    (head,) = take(1)
    before = take(2) if more else None
    out, head_out, signal, shelf = refs
    patch = head.shape[0]
    rows = shelf.shape[2]
    turn = meeting()

    @pl.when(pl.program_id(0) == 0)
    def _():
        gradient = before[1][...] if more else jnp.zeros(head_out.shape, F32)
        place = 0
        for _, sent, table in samples:
            gate, shift, scale = table[0:1, :], table[1:2, :], 1.0 + table[2:3, :]
            for ref in sent:
                block = ref[...].astype(F32)
                normed = block[:rows]
                pieces = [
                    block[r : r + 8, c : c + rows]
                    for r in range(rows, block.shape[0], 8)
                    for c in range(0, block.shape[1] - rows + 1, rows)
                ]
                sums = pieces[0] + jnp.concatenate([pieces[0][3:], pieces[0][:3]], axis=0)
                sums = sums.T
                cot = jnp.concatenate(pieces[1 : 1 + patch // 8], axis=0).astype(BF16)
                inverse, first, second = sums[:, 0:1], sums[:, 1:2], sums[:, 2:3]
                scaled = turned_dot(cot, head[...]) * scale
                grad = inverse * (scaled - first - normed * second)
                signal[place : place + rows, :] = (grad * gate).astype(BF16)
                shaped = (normed * scale + shift).astype(BF16)
                gradient = gradient + jnp.dot(cot, shaped, preferred_element_type=F32)
                place += rows
        head_out[...] = gradient

    tile = out.shape[0]
    here = pl.ds(pl.multiple_of(pl.program_id(0) * tile, tile), tile)
    wanted = [(hidden, k) for slots, (hidden, *_) in zip(counts, samples) for k in slots]
    for place, (hidden, k) in enumerate(wanted):
        for j in range(n):

            @pl.when(jnp.bitwise_xor(turn, k) == j)
            def _():
                shelf[place] = hidden[j][here, :]

    left = jnp.concatenate([shelf[place] for place in range(len(wanted))], axis=1)
    product = jnp.dot(left, signal[...], preferred_element_type=F32)
    if more:
        product = product + before[0][here, :].astype(F32)
    out[...] = product.astype(BF16)


def contract(samples, head, before=None):
    n = len(samples[0][0])
    counts = [tuple(slots) for _, slots, *_ in samples]
    tokens, depth = samples[0][0][0].shape
    width = head.shape[1]
    tile = max(t for t in range(16, min(depth, 576) + 1, 16) if depth % t == 0)
    operands, in_specs = [], []
    for hidden, slots, sent, table in samples:
        operands += [block.T for block in hidden]
        in_specs += [in_place() for _ in range(n)]
        rest = [*(sent[k] for k in slots), table]
        operands += rest
        in_specs += [whole_block(x) for x in rest]
    operands.append(head)
    in_specs.append(whole_block(head))
    if before is not None:
        operands += before
        in_specs += [in_place(), whole_block(before[1])]
    return pl.pallas_call(
        functools.partial(contract_kernel, n, counts, before is not None),
        grid=(depth // tile,),
        in_specs=in_specs,
        out_specs=[pl.BlockSpec((tile, width), lambda i: (i, 0)), whole_block(head)],
        out_shape=[
            jax.ShapeDtypeStruct((depth, width), BF16),
            jax.ShapeDtypeStruct(head.shape, F32),
        ],
        scratch_shapes=[
            pltpu.VMEM((sum(map(len, counts)) * tokens, width), BF16),
            pltpu.VMEM((sum(map(len, counts)), tile, tokens), BF16),
        ],
        compiler_params=pltpu.CompilerParams(vmem_limit_bytes=VMEM),
        cost_estimate=SHORT,
        name="contract",
    )(*operands)


def lanes(shape):
    return lax.broadcasted_iota(jnp.int32, shape, 1)


def model_stats(summed, res, table, head, cot):
    patch, rows = cot.shape
    gate, shift, scale = table[0:1, :], table[1:2, :], 1.0 + table[2:3, :]
    stream = res[...].astype(F32) + gate * summed
    scaled = turned_dot(cot.astype(BF16), head[...]) * scale
    mean = jnp.mean(stream, axis=1, keepdims=True)
    centred = stream - mean
    columns = [
        mean,
        jnp.sum(centred * centred, axis=1, keepdims=True),
        jnp.sum(scaled, axis=1, keepdims=True),
        jnp.sum(scaled * centred, axis=1, keepdims=True),
    ]
    lane = lanes((rows, rows))
    spread = jnp.zeros((rows, rows), F32)
    for place, column in enumerate(columns):
        spread = jnp.where(lane == place, column, spread)
    first = spread.T[:8]
    wide = head[...].astype(F32)
    slope = jnp.sum(wide * scale, axis=1, keepdims=True)
    offset = jnp.sum(wide * shift, axis=1, keepdims=True)
    lane, row = lanes((patch, rows)), lax.broadcasted_iota(jnp.int32, (patch, rows), 0)
    both = jnp.where(lane == row, slope, jnp.where(lane == row + patch, offset, 0.0))
    both = jnp.sum(both, axis=0, keepdims=True)
    first = jnp.where(lax.broadcasted_iota(jnp.int32, (8, rows), 0) == len(columns), both, first)
    product = lax.dot_general(
        head[...], (centred * scale).astype(BF16), (((1,), (1,)), ((), ())), preferred_element_type=F32
    )
    return stream, scaled, jnp.concatenate([first, product], axis=0)


def stats_kernel(n, *refs):
    big, guide = refs[n : n + 3], refs[n + 3 : n + 6]
    cot, strength = refs[n + 6][...], refs[n + 7][refs[n + 8][0]]
    stream_big, scaled_big, stream_guide, scaled_guide, told = refs[n + 9 :]
    summed = total([ref[...] for ref in refs[:n]])
    width = big[0].shape[1]
    stream_big[...], scaled_big[...], told_big = model_stats(summed[:, :width], *big, strength * cot)
    stream_guide[...], scaled_guide[...], told_guide = model_stats(
        summed[:, width:], *guide, (1.0 - strength) * cot
    )
    left = jnp.concatenate([told_big[:8], told_guide[:8]], axis=0)
    parts = []
    for _ in range(3):
        parts.append(left.astype(BF16).astype(F32))
        left = left - parts[-1]
    told[...] = jnp.concatenate([*parts, told_big[8:], told_guide[8:]], axis=0).astype(BF16)


def specs(arrays):
    return [pl.BlockSpec(memory_space=pltpu.VMEM) for _ in arrays] + [
        pl.BlockSpec(memory_space=pltpu.SMEM) for _ in range(2)
    ]


def local_stats(received, big, guide, cot, weight):
    patch, rows = cot.shape
    widths = [model[-1].shape[1] for model in (big, guide)]
    shapes = [(rows, w) for w in widths for _ in range(2)]
    arrays = [*received, *big, *guide, cot]
    return pl.pallas_call(
        functools.partial(stats_kernel, len(received)),
        in_specs=specs(arrays),
        out_shape=[jax.ShapeDtypeStruct(shape, F32) for shape in shapes]
        + [jax.ShapeDtypeStruct((48 + 2 * patch, rows), BF16)],
        compiler_params=pltpu.CompilerParams(vmem_limit_bytes=VMEM_NORM),
        cost_estimate=SHORT,
        name="local_stats",
    )(*arrays, *weight)


def gathered(refs):
    told = [ref[...].astype(F32) for ref in refs]
    first = [t[:16] + t[16:32] + t[32:48] for t in told]
    half = 48 + (told[0].shape[0] - 48) // 2
    return (
        ([f[:8] for f in first], [t[48:half] for t in told]),
        ([f[8:] for f in first], [t[half:] for t in told]),
    )


def model_norm(parts, stream):
    rows, width = stream.shape
    full = width * len(parts)
    centre = sum(p[0:1] for p in parts) / len(parts)
    squares = sum(p[1:2] + width * jnp.square(p[0:1] - centre) for p in parts)
    inverse = lax.rsqrt(squares / full + EPSILON)
    first = sum(p[2:3] for p in parts) / full
    second = inverse * sum(p[3:4] + (p[0:1] - centre) * p[2:3] for p in parts) / full
    sums = jnp.concatenate([inverse, first, second], axis=0)
    turned = jnp.concatenate([sums, centre, jnp.zeros((4, rows), F32)], axis=0).T
    return centre, sums, turned, (stream[...] - turned[:, 3:4]) * turned[:, 0:1]


def model_rest(parts, products, stream, scaled):
    centre, sums, turned, normed = model_norm(parts, stream)
    grad = turned[:, 0:1] * (scaled[...] - turned[:, 1:2] - normed * turned[:, 2:3])
    patch, rows = products[0].shape
    lane, row = lanes((patch, rows)), lax.broadcasted_iota(jnp.int32, (patch, rows), 0)
    out, offset = 0.0, 0.0
    for p, product in zip(parts, products):
        slope = jnp.sum(jnp.where(lane == row, p[4:5], 0.0), axis=1, keepdims=True)
        offset += jnp.sum(jnp.where(lane == row + patch, p[4:5], 0.0), axis=1, keepdims=True)
        out += product + (p[0:1] - centre) * slope
    return grad.astype(BF16), sums[0:1] * out + offset


def norm_kernel(n, *refs):
    (parts, _), _ = gathered(refs[:n])
    stream, cot, weights, which, sent = refs[n:]
    _, sums, _, normed = model_norm(parts, stream)
    rows, width = normed.shape
    high = sums.astype(BF16).astype(F32)
    pieces = [jnp.concatenate([high, sums - high, jnp.zeros((2, rows), F32)], axis=0)]
    weighted = weights[which[0]] * cot[...]
    pieces += [weighted[r : r + 8] for r in range(0, weighted.shape[0], 8)]
    across = width // rows
    lines = [normed]
    for r in range(0, len(pieces), across):
        line = pieces[r : r + across]
        line += [jnp.zeros((8, width - rows * len(line)), F32)] if width > rows * len(line) else []
        lines.append(jnp.concatenate(line, axis=1))
    sent[...] = jnp.concatenate(lines, axis=0).astype(BF16)


def whole_norm(told, stream, cot, weight):
    patch, rows = cot.shape
    width = stream.shape[1]
    below = 8 * pl.cdiv(1 + patch // 8, width // rows)
    arrays = [*told, stream, cot]
    return pl.pallas_call(
        functools.partial(norm_kernel, len(told)),
        in_specs=specs(arrays),
        out_shape=jax.ShapeDtypeStruct((rows + below, width), BF16),
        compiler_params=pltpu.CompilerParams(vmem_limit_bytes=VMEM_NORM),
        cost_estimate=SHORT,
        name="whole_norm",
    )(*arrays, *weight)


def rest_kernel(n, *refs):
    big, guide = gathered(refs[:n])
    stream_big, scaled_big, stream_guide, scaled_guide, weights, which = refs[n : n + 6]
    grad_big, grad_guide, guided = refs[n + 6 :]
    grad_big[...], out_big = model_rest(*big, stream_big, scaled_big)
    grad_guide[...], out_guide = model_rest(*guide, stream_guide, scaled_guide)
    guided[...] = out_guide + weights[which[0]] * (out_big - out_guide)


def norm_rest(told, streams, patch, weight):
    rows = told[0].shape[1]
    arrays = [*told, *streams]
    return pl.pallas_call(
        functools.partial(rest_kernel, len(told)),
        in_specs=specs(arrays),
        out_shape=[
            jax.ShapeDtypeStruct(streams[0].shape, BF16),
            jax.ShapeDtypeStruct(streams[2].shape, BF16),
            jax.ShapeDtypeStruct((patch, rows), F32),
        ],
        compiler_params=pltpu.CompilerParams(vmem_limit_bytes=VMEM_NORM),
        cost_estimate=SHORT,
        name="norm_rest",
    )(*arrays, *weight)


def shards(
    sizes,
    fc_big,
    fc_guide,
    res_big,
    res_guide,
    cotangent,
    proj_big,
    proj_guide,
    head_big,
    head_guide,
    modulation_big,
    modulation_guide,
    weight_table,
    time_index,
    weight_index,
):
    n_grp, n_seq, n_tp = sizes
    width_big, width_guide = proj_big.shape[1], proj_guide.shape[1]
    tile = next(t for t in (640, 256, 128) if width_big % t == 0)
    width_big, width_guide = proj_big.shape[1], proj_guide.shape[1]
    tile = next(t for t in (640, 256, 128) if width_big % t == 0)
    near_big, far_big = near_far(fc_big, n_seq)
    near_guide, far_guide = near_far(fc_guide, n_seq, near_big[1])
    early_big = project_early(near_big, proj_big, tile)
    far_big = forward(far_big, n_seq, early_big)
    big_blocks = near_big + far_big
    early_guide = project_early(after(near_guide, early_big), proj_guide, 128)
    fc_crossed = [swap(fc_big, "grp", n_grp, g) for g in range(1, n_grp)]
    far_guide = forward(far_guide, n_seq, (early_guide, far_big[0], fc_crossed))

    width = width_big + width_guide
    terms = project(far_big, proj_big, tile, width, early_big)
    terms = project(far_guide, proj_guide, 128, width, early_guide, terms)
    received, joined = scatter(terms, n_tp)
    begun = after((fc_crossed, modulation_big, modulation_guide), terms)
    time_late = after(time_index, terms)
    time_others = [swap(time_late, "grp", n_grp, g) for g in range(1, n_grp)]
    fc_far = [
        [block, *(swap(block, "seq", n_seq, k) for k in range(2, n_seq, 2))] for block in begun[0]
    ]
    table_big, table_guide, *tables = lookup(
        [begun[1], begun[2], *(begun[1] for _ in time_others)], [time_index, time_index, *time_others]
    )
    received, fc_far, tables, table_big, table_guide = lax.optimization_barrier(
        (received, fc_far, tables, table_big, table_guide)
    )
    fc_others = [forward(far, n_seq) for far in fc_far]
    weight = (weight_table, weight_index)

    head_big, head_guide, cot = head_big.T, head_guide.T, cotangent.T
    *streams, told = local_stats(
        received, [res_big, table_big, head_big], [res_guide, table_guide, head_guide], cot, weight
    )
    told = gather_direct(told, "seq", n_seq)
    sent = whole_norm(told, streams[0], cot, weight)
    rest = norm_rest(told, streams, cot.shape[0], weight)

    if (n_grp, n_tp) == (2, 4):
        sent_tp, crossed, rest = gather_pairs(sent, rest)
        own = (big_blocks, (0, 2, 3), sent_tp, table_big)
        other = (fc_others[0], (0, 1, 2), crossed, tables[0])
        grads = contract([own, other], head_big)
        own, other = (own[0], (1,), *own[2:]), (other[0], (3,), *other[2:])
        grads = contract([own, other], head_big, grads)
    else:
        sent_tp = gather_direct(sent, "tp", n_tp)
        every = tuple(range(n_tp))
        grads = contract([(big_blocks, every, sent_tp, table_big)], head_big)
        for g in range(1, n_grp):
            crossed = [swap(x, "grp", n_grp, g) for x in sent_tp]
            sample = (fc_others[g - 1], every, crossed, tables[g - 1])
            grads = contract([sample], head_big, grads)
    return (
        rest[2].T,
        grads[0],
        grads[1].T,
        rest[0],
        rest[1],
    )


def solution(mesh):
    sizes = tuple(mesh.shape[name] for name in ("grp", "seq", "tp"))
    placed = (
        P(("grp", "seq"), "tp"),
        P(("grp", "seq"), "tp"),
        P(("grp", "tp"), "seq"),
        P(("grp", "tp"), "seq"),
        P(("grp", "tp"), None),
        P("tp", "seq"),
        P("tp", "seq"),
        P("seq", None),
        P("seq", None),
        P(None, None, "seq"),
        P(None, None, "seq"),
        P(),
        P("grp"),
        P("grp"),
    )
    return jax.shard_map(
        functools.partial(shards, sizes),
        mesh=mesh,
        in_specs=placed,
        out_specs=(
            P(("grp", "tp"), None),
            P("tp", "seq"),
            P("seq", None),
            P(("grp", "tp"), "seq"),
            P(("grp", "tp"), "seq"),
        ),
        check_vma=False,
    )
```
